256 devices in a mesh: date: 8 (over x, core), space: 32 (over z, y).
Axes of the slice: x: 4, y: 4, z: 8, core: 2. Of those that a mesh axis runs over, the one named last changes fastest.
Arguments:
- backscatter: float32 [64, 2, 512, 2048], P('date', None, 'space'), may hold values from 0.01 to 1
- edge_dirs: int32 [64, 512, 2048], P('date', 'space'), may hold values from 0 to 7
- labels: int32 [512, 2048], P('space', 'date'), may hold values from 0 to 4095, as said below
- parcel_slot: int32 [4096], replicated, may hold values from 0 to 4095, as said below
Outputs:
- series_coeffs: bfloat16 [512, 2048, 128], P('space', 'date')
- parcel_means: float32 [4096, 128], P(('date', 'space'))
The draws below stay inside these ranges and needn't reach their ends.
Inputs may be any that keep to these rules, and one draw needn't show every extreme that they name: `labels`: each parcel's pixels form four fields, in two neighbouring row strips of 16 rows (the first starting at an even multiple of 16) and two column ranges 2048 / 2 columns apart, each range lying within one block of 256 columns (the columns of one `date` index); parcels that no pixel names may exist. `parcel_slot`: a permutation of the parcels that puts each parcel's output row on one of the four devices holding its fields (device index = date index * 32 + space index, 16 rows each).
All inputs are finite; a program needn't handle non-finite values.
Results may differ from the reference program's by a relative error of at most 0.0049.
Values may be sent and summed in bfloat16 or wider, within the bound.
A program may use at most 64 MiB of HBM per device.

```python
import math
import jax
import jax.numpy as jnp
from jax import lax

DATES = 64
POLS = 2
FEATS = 128
W = 2048
ROWS_DEV = 16
PAR_DEV = 16
H = 512
P_SIZE = 4096
DATE_DEV = 8


def parcel_layout(key):
    key = jax.random.fold_in(key, 11)
    keys = jax.random.split(key, 3)
    nspace = H // ROWS_DEV
    ndate = DATES // DATE_DEV
    width = W // ndate
    half_date = ndate // 2
    half_space = nspace // 2
    pieces = 4 * PAR_DEV
    piece_cols = width // pieces
    rows = jnp.arange(H, dtype=jnp.int32)[:, None]
    cols = jnp.arange(W, dtype=jnp.int32)[None, :]
    jitter = jax.random.randint(keys[0], (H, W), -1, 2, dtype=jnp.int32)
    local = jnp.clip(cols % width + jitter, 0, width - 1)
    within = local // piece_cols
    strip = rows // ROWS_DEV
    group = cols // width
    quad = group % half_date * half_space + strip // 2
    parcel = (quad * pieces + within).astype(jnp.int32)
    order = jax.random.permutation(keys[1], P_SIZE).astype(jnp.int32)
    sigma = jax.random.permutation(keys[2], pieces).astype(jnp.int32)
    ident = jnp.arange(P_SIZE, dtype=jnp.int32)
    rank = jnp.take(sigma, ident % pieces)
    quad_id = ident // pieces
    base_date = quad_id // half_space
    base_space = quad_id % half_space
    corner = rank // PAR_DEV
    owner_date = base_date + corner % 2 * half_date
    owner_space = 2 * base_space + corner // 2
    owner = owner_date * nspace + owner_space
    slot = (owner * PAR_DEV + rank % PAR_DEV).astype(jnp.int32)
    labels = jnp.take(order, parcel).astype(jnp.int32)
    slots = jnp.zeros((P_SIZE,), jnp.int32).at[order].set(slot)
    return (labels, slots)


def draw_labels(key, part):
    return parcel_layout(key)[0]


def draw_parcel_slot(key, part):
    return parcel_layout(key)[1]


def place_ends(entries, rng, least, top_value):
    extent = entries.shape
    index_at = [jax.random.randint(jax.random.fold_in(rng, axis), (), 0, extent[axis]) for axis in range(len(extent))]
    entries = entries.at[tuple(index_at)].set(least)
    longest = extent.index(max(extent))
    index_at[longest] = (index_at[longest] + 1) % extent[longest]
    return entries.at[tuple(index_at)].set(top_value)


def level_of(stream_key, dims, cuts, least, largest):
    def one(dim, blocks):
        draws = jax.random.uniform(jax.random.fold_in(jax.random.fold_in(stream_key, 6), dim), (blocks,), jnp.float32, least / len(cuts), largest / len(cuts))
        return jnp.repeat(jnp.exp(draws), dims[dim] // blocks).reshape((-1,) + (1,) * (len(dims) - dim - 1))

    factor_of = one(*cuts[0])
    for cut in cuts[1:]:
        factor_of = factor_of * one(*cut)
    return factor_of


def setup_inputs(seed: int = 0) -> dict:
    key_of = jax.random.split(jax.random.key(seed), 5)
    backscatter = jnp.clip(jnp.exp(math.log(1.0) - 4.6051702 * jax.random.uniform(key_of[0], (DATES, POLS, H, W), jnp.float32) ** level_of(key_of[0], (DATES, POLS, H, W), ((0, 8), (2, 32)), -0.2, 0.2)), 0.01, 1.0)
    edge_dirs = place_ends(jax.random.randint(key_of[1], (DATES, H, W), 0, 8), jax.random.fold_in(key_of[1], 1), 0, 7).astype(jnp.int32)
    labels = draw_labels(jax.random.fold_in(key_of[4], 71), 0)
    parcel_slot = draw_parcel_slot(jax.random.fold_in(key_of[4], 71), 0)
    return dict(backscatter=backscatter, edge_dirs=edge_dirs, labels=labels, parcel_slot=parcel_slot)


vectors = ((1, 0), (1, 1), (0, 1), (-1, 1), (-1, 0), (-1, -1), (0, -1), (1, -1))
speckle = 0.25

def lee_filter(padded, masks, nrows, ncols):
    first = [None] * 8
    second = [None] * 8
    for i in range(-3, 4):
        for j in range(-3, 4):
            piece = padded[..., 3 + i:3 + i + nrows, 3 + j:3 + j + ncols]
            square = piece * piece
            for d in range(8):
                if i * vectors[d][0] + j * vectors[d][1] >= 0:
                    first[d] = piece if first[d] is None else first[d] + piece
                    second[d] = square if second[d] is None else second[d] + square
    centre = padded[..., 3:3 + nrows, 3:3 + ncols]
    sel_first = jnp.zeros_like(centre)
    sel_second = jnp.zeros_like(centre)
    for d in range(8):
        hit = masks == d
        sel_first = jnp.where(hit, first[d], sel_first)
        sel_second = jnp.where(hit, second[d], sel_second)
    mean = sel_first / 28.0
    var = sel_second / 28.0 - mean * mean
    noise = speckle * mean * mean
    signal = jnp.maximum((var - noise) / (1.0 + speckle), 0.0)
    gainv = signal / (signal + noise)
    filtered = mean + gainv * (centre - mean)
    return jnp.log10(filtered).astype(jnp.bfloat16)

def make_basis(count):
    times = jnp.arange(count, dtype=jnp.float32)[:, None]
    index = jnp.arange(count, dtype=jnp.float32)[None, :]
    half = count // 2
    cosine = jnp.cos(2.0 * jnp.pi * index * times / count)
    sine = jnp.sin(2.0 * jnp.pi * (index - half) * times / count)
    table = jnp.where(index <= half, cosine, sine) * jnp.sqrt(2.0 / count)
    return table.astype(jnp.bfloat16)

def reference(backscatter, edge_dirs, labels, parcel_slot):

    def one_date(pair):
        images, masks = pair
        padded = jnp.pad(images, ((0, 0), (3, 3), (3, 3)))
        return lee_filter(padded, masks[None], H, W)
    level = lax.map(one_date, (backscatter, edge_dirs))
    basis = make_basis(DATES)
    coeffs = jnp.einsum('tprc,tj->rcpj', level.astype(jnp.float32), basis.astype(jnp.float32))
    series_coeffs = coeffs.reshape(H, W, FEATS).astype(jnp.bfloat16)
    slots = jnp.take(parcel_slot, labels.reshape(-1).astype(jnp.int32)).astype(jnp.int32)
    sums = jax.ops.segment_sum(series_coeffs.reshape(-1, FEATS).astype(jnp.float32), slots, num_segments=P_SIZE)
    counts = jax.ops.segment_sum(jnp.ones(slots.shape, jnp.float32), slots, num_segments=P_SIZE)
    parcel_means = sums / jnp.maximum(counts, 1.0)[:, None]
    return (series_coeffs, parcel_means)
```

```python
import functools

import jax
import jax.numpy as jnp
import ml_dtypes
import numpy as np
from jax import lax
from jax.experimental import pallas as pl
from jax.experimental.pallas import tpu as pltpu
from jax.sharding import PartitionSpec as P

MESH = pl.DeviceIdType.MESH
F32 = jnp.float32
BF16 = jnp.bfloat16
DATES = 64
ROWS = 16
TALL = ROWS + 6
ZERO = TALL
LOG10E = 0.4342944819032518


def basis_table(dates, group, pols):
    times = np.arange(dates, dtype=np.float32)[:, None]
    index = np.arange(dates, dtype=np.float32)[None, :]
    half = dates // 2
    scale = np.sqrt(np.float32(2.0 / dates))
    cosine = np.cos(np.float32(2.0 * np.pi) * index * times / np.float32(dates))
    sine = np.sin(np.float32(2.0 * np.pi) * (index - half) * times / np.float32(dates))
    table = (np.where(index <= half, cosine, sine) * scale).astype(np.float32)
    wide = np.zeros((dates // group, pols, group, pols, dates), np.float32)
    for p in range(pols):
        wide[:, p, :, p, :] = table.reshape(dates // group, group, dates)
    return wide.reshape(dates * pols, pols * dates).astype(ml_dtypes.bfloat16)


def kernel(
    ndate, nspace, wide,
    x_hbm, e_hbm, labels_ref, slot_ref, basis_ref,
    out_ref, means_ref,
    xin, ein, a0, r7, xp, xm, d1, d2, vv, vm, tt, p2, hh, sendbuf, got, onehot, acc, qgot,
    in_sem, halo_send, halo_recv, send_sem, recv_sem, own_sem, qsend, qrecv,
):
    full = wide + 128
    date = lax.axis_index("date")
    space = lax.axis_index("space")
    half = ndate // 2

    order = list(range(3)) + list(range(ROWS - 3, ROWS)) + list(range(3, ROWS - 3))

    def loads(r):
        for p in range(2):
            yield pltpu.make_async_copy(x_hbm.at[:, p, r, :], xin.at[r + 3, p, :, 0:wide], in_sem.at[r, p])
        yield pltpu.make_async_copy(e_hbm.at[:, r, :], ein.at[r], in_sem.at[r, 2])

    for r in order:
        for copy in loads(r):
            copy.start()

    barrier = pltpu.get_barrier_semaphore()
    for k in range(1, ndate):
        pl.semaphore_signal(barrier, inc=1, device_id={"date": lax.rem(date + k, ndate)}, device_id_type=MESH)
    mate = space + 1 - 2 * lax.rem(space, 2)
    opposite = lax.rem(date + half, ndate)
    pl.semaphore_signal(barrier, inc=1, device_id={"date": opposite, "space": mate}, device_id_type=MESH)

    @pl.when(space > 0)
    def _():
        pl.semaphore_signal(barrier, inc=1, device_id={"space": space - 1}, device_id_type=MESH)

    @pl.when(space < nspace - 1)
    def _():
        pl.semaphore_signal(barrier, inc=1, device_id={"space": space + 1}, device_id_type=MESH)

    xin[:, :, :, wide:] = jnp.zeros((TALL, 2, 8, 128), F32)
    zero_row = jnp.zeros((2, 8, full), F32)
    for q in range(2):
        a0[q, ZERO] = zero_row
        r7[q, ZERO] = zero_row[:, :, :wide]
        p2[q, ZERO] = zero_row[:, :, :wide]
    xp[ZERO] = zero_row
    xm[ZERO] = zero_row

    base_date = lax.rem(date, half)
    base_space = space - lax.rem(space, 2)
    parts = []
    for u in range(4):
        owner = (base_date + (u // 2) * half) * nspace + base_space + u % 2
        parts.append(lax.broadcasted_iota(jnp.int32, (ROWS, 128), 0) + owner * ROWS)
    ids = jnp.concatenate(parts, axis=0)
    lane = lax.broadcasted_iota(jnp.int32, (4 * ROWS, 128), 1).astype(F32)
    total = jnp.zeros((4 * ROWS, 128), F32)
    for g in range(slot_ref.shape[0]):
        total = total + jnp.where(ids == slot_ref[g : g + 1, :], lane + float(128 * g), 0.0)
    parcel_of = jnp.sum(total, axis=1, keepdims=True).astype(jnp.int32)
    for r in range(ROWS):
        onehot[r] = jnp.where(parcel_of == labels_ref[r : r + 1, :], 1.0, 0.0).astype(BF16)

    def down():
        return pltpu.make_async_remote_copy(
            src_ref=xin.at[ROWS : ROWS + 3, :, :, 0:wide], dst_ref=xin.at[0:3, :, :, 0:wide],
            send_sem=halo_send.at[0], recv_sem=halo_recv.at[0],
            device_id={"space": space + 1}, device_id_type=MESH)

    def up():
        return pltpu.make_async_remote_copy(
            src_ref=xin.at[3:6, :, :, 0:wide], dst_ref=xin.at[ROWS + 3 : ROWS + 6, :, :, 0:wide],
            send_sem=halo_send.at[1], recv_sem=halo_recv.at[1],
            device_id={"space": space - 1}, device_id_type=MESH)

    degree = (ndate - 1) + 1 + jnp.where(space > 0, 1, 0) + jnp.where(space < nspace - 1, 1, 0)
    pl.semaphore_wait(barrier, degree)
    for r in list(range(3)) + list(range(ROWS - 3, ROWS)):
        for copy in loads(r):
            copy.wait()

    @pl.when(space < nspace - 1)
    def _():
        down().start()

    @pl.when(space > 0)
    def _():
        up().start()

    @pl.when(space == 0)
    def _():
        xin[0:3, :, :, 0:wide] = jnp.zeros((3, 2, 8, wide), F32)

    @pl.when(space == nspace - 1)
    def _():
        xin[ROWS + 3 : ROWS + 6, :, :, 0:wide] = jnp.zeros((3, 2, 8, wide), F32)

    def send(r):
        for k in range(1, ndate):
            peer = lax.rem(date + k, ndate)
            pltpu.make_async_remote_copy(
                src_ref=sendbuf.at[r, peer], dst_ref=got.at[r, date],
                send_sem=send_sem, recv_sem=recv_sem.at[r],
                device_id={"date": peer}, device_id_type=MESH).start()
        pltpu.make_async_copy(sendbuf.at[r, date], got.at[r, date], own_sem.at[r]).start()

    def left(v, n):
        return pltpu.roll(v, full - n, axis=1)

    def right(v, n):
        return pltpu.roll(v, n, axis=1)

    def back(i, s, n):
        return jnp.where(i - n >= s, i - n, ZERO)

    def phase1(i, s, fresh, emit):
        lo = back(i, s, 7)
        new = lax.rem(i, 2)
        old = 1 - new
        for p in range(2):
            if fresh:
                x = xin[i, p]
                for q in range(2):
                    v = x * x if q else x
                    pair = v + left(v, 1)
                    four = pair + left(pair, 2)
                    a0[q, i, p] = four
                    r7[q, i, p] = (four + right(four, 3) - v)[:, :wide]
                xp[i, p] = left(x, 3)
                xm[i, p] = right(x, 3)
            for q in range(2):
                def sq(v):
                    return v * v if q else v

                d1[new, q, p] = left(d1[old, q, p] - sq(xp[lo, p]), 1) + sq(xm[i, p])
                d2[new, q, p] = right(d2[old, q, p] - sq(xm[lo, p]), 1) + sq(xp[i, p])
                v = vv[q, p] + (a0[q, i, p] - a0[q, lo, p])
                vv[q, p] = v
                if emit:
                    vm[q, p] = right(v, 3)[:, :wide]

    def phase2(i, s, emit):
        lo = back(i, s, 7)
        new = lax.rem(i, 2)
        old = 1 - new
        r = i - 6
        for c in range(ndate):
            width = wide // ndate
            cols = slice(c * width, (c + 1) * width)
            if emit:
                e = ein[r, :, cols]
                b0 = ((e & 1) > 0)[None]
                b1 = ((e & 2) > 0)[None]
                b2 = ((e & 4) > 0)[None]
            sums = []
            for q in range(2):
                rn = r7[q, i, :, :, cols]
                ro = r7[q, lo, :, :, cols]
                d1n, d1o = d1[new, q, :, :, cols], d1[old, q, :, :, cols]
                d2n, d2o = d2[new, q, :, :, cols], d2[old, q, :, :, cols]
                t1 = tt[q, 0, :, :, cols] - d1o + rn
                t3 = tt[q, 1, :, :, cols] + d2n - ro
                t5 = tt[q, 2, :, :, cols] + d1n - ro
                t7 = tt[q, 3, :, :, cols] - d2o + rn
                pr = rn + r7[q, back(i, s, 1), :, :, cols]
                h = pr + p2[q, back(i, s, 2), :, :, cols]
                tt[q, 0, :, :, cols] = t1
                tt[q, 1, :, :, cols] = t3
                tt[q, 2, :, :, cols] = t5
                tt[q, 3, :, :, cols] = t7
                p2[q, i, :, :, cols] = pr
                hh[q, i, :, :, cols] = h
                if emit:
                    s02 = jnp.where(b1, vv[q, :, :, cols], h)
                    s46 = jnp.where(b1, vm[q, :, :, cols], hh[q, i - 3, :, :, cols])
                    s13 = jnp.where(b1, t3, t1)
                    s57 = jnp.where(b1, t7, t5)
                    sums.append(jnp.where(b2, jnp.where(b0, s57, s46), jnp.where(b0, s13, s02)))
            if emit:
                first, second = sums
                x = xin[i - 3, :, :, cols]
                mean = first * (1.0 / 28.0)
                sq_mean = mean * mean
                excess = jnp.maximum(second * (1.0 / 28.0) - 1.25 * sq_mean, 0.0)
                under = excess + 0.3125 * sq_mean
                inv = pl.reciprocal(under, approx=True)
                inv = inv * (2.0 - under * inv)
                filtered = mean + excess * inv * (x - mean)
                level = jnp.log(filtered) * LOG10E
                sendbuf[r, c] = level.reshape(2 * 8, width).astype(BF16)

    def reset():
        d1[...] = jnp.zeros(d1.shape, F32)
        d2[...] = jnp.zeros(d2.shape, F32)
        vv[...] = jnp.zeros(vv.shape, F32)
        tt[...] = jnp.zeros(tt.shape, F32)

    def step(s, fresh, emit):
        def body(i, carry):
            if fresh and s == 3:
                @pl.when(jnp.logical_and(i >= 6, i < ROWS))
                def _():
                    for copy in loads(i - 3):
                        copy.wait()
            phase1(i, s, fresh, emit)
            phase2(i, s, emit)
            if emit:
                send(i - 6)
            return carry

        return body

    reset()
    lax.fori_loop(3, 9, step(3, True, False), 0)
    lax.fori_loop(9, ROWS + 3, step(3, True, True), 0)

    @pl.when(space < nspace - 1)
    def _():
        up().wait_recv()

    lax.fori_loop(ROWS + 3, ROWS + 6, step(3, True, True), 0)

    @pl.when(space > 0)
    def _():
        down().wait_recv()

    reset()
    lax.fori_loop(0, 3, step(0, True, False), 0)
    lax.fori_loop(3, 6, step(0, False, False), 0)
    lax.fori_loop(6, 9, step(0, False, True), 0)

    acc[...] = jnp.zeros(acc.shape, F32)
    ones = jnp.ones((wide // ndate, 128), BF16)

    def fit(r):
        pltpu.make_async_copy(got.at[r, 0 : ndate - 1], got.at[r, 0 : ndate - 1], recv_sem.at[r]).wait()
        pltpu.make_async_copy(sendbuf.at[r, date], got.at[r, date], own_sem.at[r]).wait()
        series = got[r].reshape(ndate * 16, wide // ndate)
        coeffs = lax.dot_general(series, basis_ref[...], (((0,), (0,)), ((), ())), preferred_element_type=F32)
        coeffs = coeffs.astype(BF16)
        out_ref[r] = coeffs
        acc[...] += jnp.dot(onehot[r], jnp.concatenate([coeffs, ones], axis=1), preferred_element_type=F32)

    def fit_step(n, carry):
        fit(lax.rem(n + 3, ROWS))
        return carry

    lax.fori_loop(0, ROWS, fit_step, 0)

    high = date // half
    low = lax.rem(space, 2)
    copies = []
    for k in range(1, 4):
        far, near = k // 2, k % 2
        part = lax.rem(high + far, 2) * 2 + lax.rem(low + near, 2)
        copy = pltpu.make_async_remote_copy(
            src_ref=acc.at[pl.ds(pl.multiple_of(part * ROWS, ROWS), ROWS)], dst_ref=qgot.at[k - 1],
            send_sem=qsend.at[k - 1], recv_sem=qrecv.at[k - 1],
            device_id={"date": opposite if far else date, "space": mate if near else space}, device_id_type=MESH)
        copy.start()
        copies.append(copy)
    total = acc[pl.ds(pl.multiple_of((high * 2 + low) * ROWS, ROWS), ROWS), :]
    for k, copy in enumerate(copies):
        copy.wait_recv()
        total = total + qgot[k]
    means_ref[...] = total[:, :128] / jnp.maximum(total[:, 128:], 1.0)

    for copy in copies:
        copy.wait_send()
    pltpu.make_async_copy(sendbuf.at[:, 0 : ndate - 1], sendbuf.at[:, 0 : ndate - 1], send_sem).wait()

    @pl.when(space < nspace - 1)
    def _():
        down().wait_send()

    @pl.when(space > 0)
    def _():
        up().wait_send()


def solution(mesh):
    ndate, nspace = mesh.shape["date"], mesh.shape["space"]
    basis = basis_table(DATES, DATES // ndate, 2)

    def local(backscatter, edge_dirs, labels, parcel_slot):
        wide = backscatter.shape[3]
        full = wide + 128
        cols = wide // ndate
        any_spec = pl.BlockSpec(memory_space=pl.ANY)
        vmem = pl.BlockSpec(memory_space=pltpu.VMEM)
        return pl.pallas_call(
            functools.partial(kernel, ndate, nspace, wide),
            out_shape=(
                jax.ShapeDtypeStruct((ROWS, cols, 128), BF16),
                jax.ShapeDtypeStruct((ROWS, 128), F32),
            ),
            in_specs=[any_spec, any_spec, vmem, vmem, vmem],
            out_specs=(vmem, vmem),
            scratch_shapes=[
                pltpu.VMEM((TALL, 2, 8, full), F32),
                pltpu.VMEM((ROWS, 8, wide), jnp.int32),
                pltpu.VMEM((2, TALL + 1, 2, 8, full), F32),
                pltpu.VMEM((2, TALL + 1, 2, 8, wide), F32),
                pltpu.VMEM((TALL + 1, 2, 8, full), F32),
                pltpu.VMEM((TALL + 1, 2, 8, full), F32),
                pltpu.VMEM((2, 2, 2, 8, full), F32),
                pltpu.VMEM((2, 2, 2, 8, full), F32),
                pltpu.VMEM((2, 2, 8, full), F32),
                pltpu.VMEM((2, 2, 8, wide), F32),
                pltpu.VMEM((2, 4, 2, 8, wide), F32),
                pltpu.VMEM((2, TALL + 1, 2, 8, wide), F32),
                pltpu.VMEM((2, TALL, 2, 8, wide), F32),
                pltpu.VMEM((ROWS, ndate, 16, cols), BF16),
                pltpu.VMEM((ROWS, ndate, 16, cols), BF16),
                pltpu.VMEM((ROWS, 4 * ROWS, cols), BF16),
                pltpu.VMEM((4 * ROWS, 256), F32),
                pltpu.VMEM((3, ROWS, 256), F32),
                pltpu.SemaphoreType.DMA((ROWS, 3)),
                pltpu.SemaphoreType.DMA((2,)),
                pltpu.SemaphoreType.DMA((2,)),
                pltpu.SemaphoreType.DMA,
                pltpu.SemaphoreType.DMA((ROWS,)),
                pltpu.SemaphoreType.DMA((ROWS,)),
                pltpu.SemaphoreType.DMA((3,)),
                pltpu.SemaphoreType.DMA((3,)),
            ],
            compiler_params=pltpu.CompilerParams(
                collective_id=0, has_side_effects=True, vmem_limit_bytes=56 * 1024 * 1024
            ),
        )(backscatter, edge_dirs, labels, parcel_slot.reshape(-1, 128), jnp.asarray(basis))

    return jax.shard_map(
        local,
        mesh=mesh,
        in_specs=(P("date", None, "space", None), P("date", "space", None), P("space", "date"), P()),
        out_specs=(P("space", "date", None), P(("date", "space"), None)),
        check_vma=False,
    )
```

```python
import functools

import jax
import jax.numpy as jnp
import ml_dtypes
import numpy as np
from jax import lax
from jax.experimental import pallas as pl
from jax.experimental.pallas import tpu as pltpu
from jax.sharding import PartitionSpec as P

MESH = pl.DeviceIdType.MESH
F32 = jnp.float32
BF16 = jnp.bfloat16
DATES = 64
ROWS = 16
TALL = ROWS + 6
ZERO = TALL
LOG10E = 0.4342944819032518
LEFT = 24
TALLER = LEFT + 256 + 24


def basis_table(dates, group, pols):
    times = np.arange(dates, dtype=np.float32)[:, None]
    index = np.arange(dates, dtype=np.float32)[None, :]
    half = dates // 2
    scale = np.sqrt(np.float32(2.0 / dates))
    cosine = np.cos(np.float32(2.0 * np.pi) * index * times / np.float32(dates))
    sine = np.sin(np.float32(2.0 * np.pi) * (index - half) * times / np.float32(dates))
    table = (np.where(index <= half, cosine, sine) * scale).astype(np.float32)
    wide = np.zeros((dates // group, pols, group, pols, dates), np.float32)
    for p in range(pols):
        wide[:, p, :, p, :] = table.reshape(dates // group, group, dates)
    return wide.reshape(dates * pols, pols * dates).astype(ml_dtypes.bfloat16)


def kernel(
    ndate, nspace, wide,
    x_hbm, e_hbm, labels_ref, slot_ref, basis_ref,
    out_ref, means_ref,
    xin, ein, yy, a0, r7, c7, tt, vv, p2, hh, ey, sendbuf, got, onehot, acc, qgot,
    in_sem, halo_send, halo_recv, send_sem, recv_sem, own_sem, qsend, qrecv,
):
    date = lax.axis_index("date")
    space = lax.axis_index("space")
    half = ndate // 2

    order = list(range(3)) + list(range(ROWS - 3, ROWS)) + list(range(3, ROWS - 3))

    def loads(r):
        for p in range(2):
            yield pltpu.make_async_copy(x_hbm.at[:, p, r, :], xin.at[r + 3, p], in_sem.at[r, p])
        yield pltpu.make_async_copy(e_hbm.at[:, r, :], ein.at[r], in_sem.at[r, 2])

    for r in order:
        for copy in loads(r):
            copy.start()

    barrier = pltpu.get_barrier_semaphore()
    for k in range(1, ndate):
        pl.semaphore_signal(barrier, inc=1, device_id={"date": lax.rem(date + k, ndate)}, device_id_type=MESH)
    mate = space + 1 - 2 * lax.rem(space, 2)
    opposite = lax.rem(date + half, ndate)
    pl.semaphore_signal(barrier, inc=1, device_id={"date": opposite, "space": mate}, device_id_type=MESH)

    @pl.when(space > 0)
    def _():
        pl.semaphore_signal(barrier, inc=1, device_id={"space": space - 1}, device_id_type=MESH)

    @pl.when(space < nspace - 1)
    def _():
        pl.semaphore_signal(barrier, inc=1, device_id={"space": space + 1}, device_id_type=MESH)

    for q in range(2):
        for ref in (yy, a0, r7):
            ref[q, ZERO] = jnp.zeros((TALLER, 128), F32)
        p2[q, ZERO] = jnp.zeros((256, 128), F32)
    yy[:, :, 0 : LEFT - 16, :] = jnp.zeros((2, TALL + 1, LEFT - 16, 128), F32)
    yy[:, :, LEFT + 272 :, :] = jnp.zeros((2, TALL + 1, TALLER - LEFT - 272, 128), F32)
    a0[:, :, 0 : LEFT - 16, :] = jnp.zeros((2, TALL + 1, LEFT - 16, 128), F32)

    base_date = lax.rem(date, half)
    base_space = space - lax.rem(space, 2)
    parts = []
    for u in range(4):
        owner = (base_date + (u // 2) * half) * nspace + base_space + u % 2
        parts.append(lax.broadcasted_iota(jnp.int32, (ROWS, 128), 0) + owner * ROWS)
    ids = jnp.concatenate(parts, axis=0)
    lane = lax.broadcasted_iota(jnp.int32, (4 * ROWS, 128), 1).astype(F32)
    total = jnp.zeros((4 * ROWS, 128), F32)
    for g in range(slot_ref.shape[0]):
        total = total + jnp.where(ids == slot_ref[g : g + 1, :], lane + float(128 * g), 0.0)
    parcel_of = jnp.sum(total, axis=1, keepdims=True).astype(jnp.int32)
    for r in range(ROWS):
        onehot[r] = jnp.where(parcel_of == labels_ref[r : r + 1, :], 1.0, 0.0).astype(BF16)

    def down():
        return pltpu.make_async_remote_copy(
            src_ref=xin.at[ROWS : ROWS + 3], dst_ref=xin.at[0:3],
            send_sem=halo_send.at[0], recv_sem=halo_recv.at[0],
            device_id={"space": space + 1}, device_id_type=MESH)

    def up():
        return pltpu.make_async_remote_copy(
            src_ref=xin.at[3:6], dst_ref=xin.at[ROWS + 3 : ROWS + 6],
            send_sem=halo_send.at[1], recv_sem=halo_recv.at[1],
            device_id={"space": space - 1}, device_id_type=MESH)

    degree = (ndate - 1) + 1 + jnp.where(space > 0, 1, 0) + jnp.where(space < nspace - 1, 1, 0)
    pl.semaphore_wait(barrier, degree)
    for r in list(range(3)) + list(range(ROWS - 3, ROWS)):
        for copy in loads(r):
            copy.wait()

    @pl.when(space < nspace - 1)
    def _():
        down().start()

    @pl.when(space > 0)
    def _():
        up().start()

    @pl.when(space == 0)
    def _():
        xin[0:3] = jnp.zeros((3, 2, 8, wide), F32)

    @pl.when(space == nspace - 1)
    def _():
        xin[ROWS + 3 : ROWS + 6] = jnp.zeros((3, 2, 8, wide), F32)

    def send(r):
        for k in range(1, ndate):
            peer = lax.rem(date + k, ndate)
            pltpu.make_async_remote_copy(
                src_ref=sendbuf.at[r, peer], dst_ref=got.at[r, date],
                send_sem=send_sem, recv_sem=recv_sem.at[r],
                device_id={"date": peer}, device_id_type=MESH).start()
        pltpu.make_async_copy(sendbuf.at[r, date], got.at[r, date], own_sem.at[r]).start()

    def back(i, s, n):
        return jnp.where(i - n >= s, i - n, ZERO)

    lanes = lax.broadcasted_iota(jnp.int32, (16, 128), 1)
    width = wide // ndate

    def spread(i):
        halves = []
        for h in range(2):
            tiles = [xin[i, p, :, b * width + h * 128 : b * width + (h + 1) * 128] for b in range(ndate) for p in range(2)]
            half_row = jnp.concatenate(tiles, axis=0).T
            yy[0, i, LEFT + h * 128 : LEFT + (h + 1) * 128] = half_row
            halves.append(half_row)
        before = pltpu.roll(halves[1][112:], 16, axis=1)
        after = pltpu.roll(halves[0][:16], 112, axis=1)
        yy[0, i, LEFT - 16 : LEFT] = jnp.where(lanes >= 16, before, 0.0)
        yy[0, i, LEFT + 256 : LEFT + 272] = jnp.where(lanes < 112, after, 0.0)
        for n in range(4):
            at = slice(LEFT - 16 + n * 72, LEFT - 16 + (n + 1) * 72)
            x = yy[0, i, at]
            yy[1, i, at] = x * x
        for q in range(2):
            for n in range(4):
                at = LEFT - 16 + n * 72
                x = yy[q, i, at : at + 72]
                four = (x + yy[q, i, at + 1 : at + 73]) + (yy[q, i, at + 2 : at + 74] + yy[q, i, at + 3 : at + 75])
                a0[q, i, at : at + 72] = four
                r7[q, i, at : at + 72] = four + a0[q, i, at - 3 : at + 69] - x

    def columns(i, s):
        lo = back(i, s, 7)
        new = lax.rem(i, 2)
        for q in range(2):
            for n in range(4):
                at = slice(LEFT - 16 + n * 72, LEFT - 16 + (n + 1) * 72)
                c7[new, q, at] = c7[1 - new, q, at] + (yy[q, i, at] - yy[q, lo, at])
            for n in range(3):
                at = slice(LEFT - 8 + n * 88, LEFT - 8 + (n + 1) * 88)
                vv[q, at] = vv[q, at] + (a0[q, i, at] - a0[q, lo, at])

    def rising(i, lo, q, at, size):
        new = lax.rem(i, 2)
        old = 1 - new
        t1 = tt[old, q, 0, at + 1 : at + 1 + size] - c7[old, q, at + 4 : at + 4 + size] + r7[q, i, at : at + size]
        t5 = tt[old, q, 2, at + 1 : at + 1 + size] - r7[q, lo, at + 1 : at + 1 + size] + c7[new, q, at - 3 : at - 3 + size]
        tt[new, q, 0, at : at + size] = t1
        tt[new, q, 2, at : at + size] = t5
        return t1, t5

    def falling(i, lo, q, at, size):
        new = lax.rem(i, 2)
        old = 1 - new
        t3 = tt[old, q, 1, at - 1 : at - 1 + size] - r7[q, lo, at - 1 : at - 1 + size] + c7[new, q, at + 3 : at + 3 + size]
        t7 = tt[old, q, 3, at - 1 : at - 1 + size] - c7[old, q, at - 4 : at - 4 + size] + r7[q, i, at : at + size]
        tt[new, q, 1, at : at + size] = t3
        tt[new, q, 3, at : at + size] = t7
        return t3, t7

    def refresh(i):
        last = 1 - lax.rem(i, 2)
        for q in range(2):
            for k in (0, 2):
                own = tt[last, q, k, LEFT + 256 : LEFT + 264]
                other = pltpu.roll(tt[last, q, k, LEFT : LEFT + 8], 112, axis=1)
                tt[last, q, k, LEFT + 256 : LEFT + 264] = jnp.where(lanes[:8] < 112, other, own)
            for k in (1, 3):
                own = tt[last, q, k, LEFT - 8 : LEFT]
                other = pltpu.roll(tt[last, q, k, LEFT + 248 : LEFT + 256], 16, axis=1)
                tt[last, q, k, LEFT - 8 : LEFT] = jnp.where(lanes[:8] >= 16, other, own)

    size = 64

    def windows(i, s, emit):
        lo = back(i, s, 7)
        r = i - 6
        if emit:
            for h in range(2):
                tiles = [ein[r, :, b * width + h * 128 : b * width + (h + 1) * 128] for b in range(ndate) for p in range(2)]
                ey[h * 128 : (h + 1) * 128] = jnp.concatenate(tiles, axis=0).T
        for q in range(2):
            rising(i, lo, q, LEFT + 256, 8)
            falling(i, lo, q, LEFT - 8, 8)
        levels = []
        for n in range(256 // size):
            at = LEFT + n * size
            here = slice(at, at + size)
            plain = slice(n * size, (n + 1) * size)
            if emit:
                e = ey[plain]
                b0 = (e & 1) > 0
                b1 = (e & 2) > 0
                b2 = e > 3
            sums = []
            for q in range(2):
                t1, t5 = rising(i, lo, q, at, size)
                t3, t7 = falling(i, lo, q, at, size)
                pair = r7[q, i, here] + r7[q, back(i, s, 1), here]
                h = pair + p2[q, back(i, s, 2), plain]
                p2[q, i, plain] = pair
                hh[q, i, plain] = h
                if emit:
                    s02 = jnp.where(b1, vv[q, here], h)
                    s46 = jnp.where(b1, vv[q, at - 3 : at - 3 + size], hh[q, i - 3, plain])
                    s13 = jnp.where(b1, t3, t1)
                    s57 = jnp.where(b1, t7, t5)
                    sums.append(jnp.where(b2, jnp.where(b0, s57, s46), jnp.where(b0, s13, s02)))
            if emit:
                first, second = sums
                x = yy[0, i - 3, here]
                mean = first * (1.0 / 28.0)
                sq_mean = mean * mean
                excess = jnp.maximum(second * (1.0 / 28.0) - 1.25 * sq_mean, 0.0)
                under = excess + 0.3125 * sq_mean
                inv = pl.reciprocal(under, approx=True)
                inv = inv * (2.0 - under * inv)
                filtered = mean + excess * inv * (x - mean)
                levels.append(jnp.log(filtered) * LOG10E)
        if emit:
            for h in range(2):
                part = jnp.concatenate(levels[h * 128 // size : (h + 1) * 128 // size], axis=0).T
                sendbuf[r, :, :, h * 128 : (h + 1) * 128] = part.astype(BF16).reshape(ndate, 16, 128)

    def reset():
        c7[...] = jnp.zeros(c7.shape, F32)
        vv[...] = jnp.zeros(vv.shape, F32)
        tt[...] = jnp.zeros(tt.shape, F32)

    def step(s, fresh, emit):
        def body(i, carry):
            if fresh and s == 3:
                @pl.when(jnp.logical_and(i >= 6, i < ROWS))
                def _():
                    for copy in loads(i - 3):
                        copy.wait()
            if fresh:
                spread(i)

            @pl.when(jnp.logical_and(lax.rem(i - s, 8) == 0, i > s))
            def _():
                refresh(i)

            columns(i, s)
            windows(i, s, emit)
            if emit:
                send(i - 6)
            return carry

        return body

    reset()
    lax.fori_loop(3, 9, step(3, True, False), 0)
    lax.fori_loop(9, ROWS + 3, step(3, True, True), 0)

    @pl.when(space < nspace - 1)
    def _():
        up().wait_recv()

    lax.fori_loop(ROWS + 3, ROWS + 6, step(3, True, True), 0)

    @pl.when(space > 0)
    def _():
        down().wait_recv()

    reset()
    lax.fori_loop(0, 3, step(0, True, False), 0)
    lax.fori_loop(3, 6, step(0, False, False), 0)
    lax.fori_loop(6, 9, step(0, False, True), 0)

    acc[...] = jnp.zeros(acc.shape, F32)
    ones = jnp.ones((wide // ndate, 128), BF16)

    def fit(r):
        pltpu.make_async_copy(got.at[r, 0 : ndate - 1], got.at[r, 0 : ndate - 1], recv_sem.at[r]).wait()
        pltpu.make_async_copy(sendbuf.at[r, date], got.at[r, date], own_sem.at[r]).wait()
        series = got[r].reshape(ndate * 16, wide // ndate)
        coeffs = lax.dot_general(series, basis_ref[...], (((0,), (0,)), ((), ())), preferred_element_type=F32)
        coeffs = coeffs.astype(BF16)
        out_ref[r] = coeffs
        acc[...] += jnp.dot(onehot[r], jnp.concatenate([coeffs, ones], axis=1), preferred_element_type=F32)

    def fit_step(n, carry):
        fit(lax.rem(n + 3, ROWS))
        return carry

    lax.fori_loop(0, ROWS, fit_step, 0)

    high = date // half
    low = lax.rem(space, 2)
    copies = []
    for k in range(1, 4):
        far, near = k // 2, k % 2
        part = lax.rem(high + far, 2) * 2 + lax.rem(low + near, 2)
        copy = pltpu.make_async_remote_copy(
            src_ref=acc.at[pl.ds(pl.multiple_of(part * ROWS, ROWS), ROWS)], dst_ref=qgot.at[k - 1],
            send_sem=qsend.at[k - 1], recv_sem=qrecv.at[k - 1],
            device_id={"date": opposite if far else date, "space": mate if near else space}, device_id_type=MESH)
        copy.start()
        copies.append(copy)
    total = acc[pl.ds(pl.multiple_of((high * 2 + low) * ROWS, ROWS), ROWS), :]
    for k, copy in enumerate(copies):
        copy.wait_recv()
        total = total + qgot[k]
    means_ref[...] = total[:, :128] / jnp.maximum(total[:, 128:], 1.0)

    for copy in copies:
        copy.wait_send()
    pltpu.make_async_copy(sendbuf.at[:, 0 : ndate - 1], sendbuf.at[:, 0 : ndate - 1], send_sem).wait()

    @pl.when(space < nspace - 1)
    def _():
        down().wait_send()

    @pl.when(space > 0)
    def _():
        up().wait_send()


def solution(mesh):
    ndate, nspace = mesh.shape["date"], mesh.shape["space"]
    basis = basis_table(DATES, DATES // ndate, 2)

    def local(backscatter, edge_dirs, labels, parcel_slot):
        wide = backscatter.shape[3]
        cols = wide // ndate
        any_spec = pl.BlockSpec(memory_space=pl.ANY)
        vmem = pl.BlockSpec(memory_space=pltpu.VMEM)
        return pl.pallas_call(
            functools.partial(kernel, ndate, nspace, wide),
            out_shape=(
                jax.ShapeDtypeStruct((ROWS, cols, 128), BF16),
                jax.ShapeDtypeStruct((ROWS, 128), F32),
            ),
            in_specs=[any_spec, any_spec, vmem, vmem, vmem],
            out_specs=(vmem, vmem),
            scratch_shapes=[
                pltpu.VMEM((TALL, 2, 8, wide), F32),
                pltpu.VMEM((ROWS, 8, wide), jnp.int32),
                pltpu.VMEM((2, TALL + 1, TALLER, 128), F32),
                pltpu.VMEM((2, TALL + 1, TALLER, 128), F32),
                pltpu.VMEM((2, TALL + 1, TALLER, 128), F32),
                pltpu.VMEM((2, 2, TALLER, 128), F32),
                pltpu.VMEM((2, 2, 4, TALLER, 128), F32),
                pltpu.VMEM((2, TALLER, 128), F32),
                pltpu.VMEM((2, TALL + 1, 256, 128), F32),
                pltpu.VMEM((2, TALL, 256, 128), F32),
                pltpu.VMEM((256, 128), jnp.int32),
                pltpu.VMEM((ROWS, ndate, 16, cols), BF16),
                pltpu.VMEM((ROWS, ndate, 16, cols), BF16),
                pltpu.VMEM((ROWS, 4 * ROWS, cols), BF16),
                pltpu.VMEM((4 * ROWS, 256), F32),
                pltpu.VMEM((3, ROWS, 256), F32),
                pltpu.SemaphoreType.DMA((ROWS, 3)),
                pltpu.SemaphoreType.DMA((2,)),
                pltpu.SemaphoreType.DMA((2,)),
                pltpu.SemaphoreType.DMA,
                pltpu.SemaphoreType.DMA((ROWS,)),
                pltpu.SemaphoreType.DMA((ROWS,)),
                pltpu.SemaphoreType.DMA((3,)),
                pltpu.SemaphoreType.DMA((3,)),
            ],
            compiler_params=pltpu.CompilerParams(
                collective_id=0, has_side_effects=True, vmem_limit_bytes=56 * 1024 * 1024
            ),
        )(backscatter, edge_dirs, labels, parcel_slot.reshape(-1, 128), jnp.asarray(basis))

    return jax.shard_map(
        local,
        mesh=mesh,
        in_specs=(P("date", None, "space", None), P("date", "space", None), P("space", "date"), P()),
        out_specs=(P("space", "date", None), P(("date", "space"), None)),
        check_vma=False,
    )
```

```python
import functools

import jax
import jax.numpy as jnp
import ml_dtypes
import numpy as np
from jax import lax
from jax.experimental import pallas as pl
from jax.experimental.pallas import tpu as pltpu
from jax.sharding import PartitionSpec as P

MESH = pl.DeviceIdType.MESH
F32 = jnp.float32
BF16 = jnp.bfloat16
DATES = 64
ROWS = 16
TALL = ROWS + 6
GROUP = 5
LOG10E = 0.4342944819032518
LEFT = 24
TALLER = LEFT + 256 + 24


def basis_table(dates, group, pols):
    times = np.arange(dates, dtype=np.float32)[:, None]
    index = np.arange(dates, dtype=np.float32)[None, :]
    half = dates // 2
    scale = np.sqrt(np.float32(2.0 / dates))
    cosine = np.cos(np.float32(2.0 * np.pi) * index * times / np.float32(dates))
    sine = np.sin(np.float32(2.0 * np.pi) * (index - half) * times / np.float32(dates))
    table = (np.where(index <= half, cosine, sine) * scale).astype(np.float32)
    wide = np.zeros((dates // group, pols, group, pols, dates), np.float32)
    for p in range(pols):
        wide[:, p, :, p, :] = table.reshape(dates // group, group, dates)
    return wide.reshape(dates * pols, pols * dates).astype(ml_dtypes.bfloat16)


def kernel(
    ndate, nspace, wide,
    x_hbm, e_hbm, labels_ref, slot_ref, basis_ref,
    out_ref, means_ref,
    xin, ein, yy, a0, r7, dd, ff, ahead, behind, ey, sendbuf, got, onehot, acc, qgot,
    in_sem, halo_send, halo_recv, send_sem, recv_sem, own_sem, qsend, qrecv,
):
    date = lax.axis_index("date")
    space = lax.axis_index("space")
    half = ndate // 2

    order = list(range(3)) + list(range(ROWS - 3, ROWS)) + list(range(3, ROWS - 3))

    def loads(r):
        for p in range(2):
            yield pltpu.make_async_copy(x_hbm.at[:, p, r, :], xin.at[r + 3, p], in_sem.at[r, p])
        yield pltpu.make_async_copy(e_hbm.at[:, r, :], ein.at[r], in_sem.at[r, 2])

    for r in order:
        for copy in loads(r):
            copy.start()

    barrier = pltpu.get_barrier_semaphore()
    for k in range(1, ndate):
        pl.semaphore_signal(barrier, inc=1, device_id={"date": lax.rem(date + k, ndate)}, device_id_type=MESH)
    mate = space + 1 - 2 * lax.rem(space, 2)
    opposite = lax.rem(date + half, ndate)
    pl.semaphore_signal(barrier, inc=1, device_id={"date": opposite, "space": mate}, device_id_type=MESH)

    @pl.when(space > 0)
    def _():
        pl.semaphore_signal(barrier, inc=1, device_id={"space": space - 1}, device_id_type=MESH)

    @pl.when(space < nspace - 1)
    def _():
        pl.semaphore_signal(barrier, inc=1, device_id={"space": space + 1}, device_id_type=MESH)

    base_date = lax.rem(date, half)
    base_space = space - lax.rem(space, 2)
    parts = []
    for u in range(4):
        owner = (base_date + (u // 2) * half) * nspace + base_space + u % 2
        parts.append(lax.broadcasted_iota(jnp.int32, (ROWS, 128), 0) + owner * ROWS)
    ids = jnp.concatenate(parts, axis=0)
    lane = lax.broadcasted_iota(jnp.int32, (4 * ROWS, 128), 1).astype(F32)
    total = jnp.zeros((4 * ROWS, 128), F32)
    for g in range(slot_ref.shape[0]):
        total = total + jnp.where(ids == slot_ref[g : g + 1, :], lane + float(128 * g), 0.0)
    parcel_of = jnp.sum(total, axis=1, keepdims=True).astype(jnp.int32)
    for r in range(ROWS):
        onehot[r] = jnp.where(parcel_of == labels_ref[r : r + 1, :], 1.0, 0.0).astype(BF16)

    def down():
        return pltpu.make_async_remote_copy(
            src_ref=xin.at[ROWS : ROWS + 3], dst_ref=xin.at[0:3],
            send_sem=halo_send.at[0], recv_sem=halo_recv.at[0],
            device_id={"space": space + 1}, device_id_type=MESH)

    def up():
        return pltpu.make_async_remote_copy(
            src_ref=xin.at[3:6], dst_ref=xin.at[ROWS + 3 : ROWS + 6],
            send_sem=halo_send.at[1], recv_sem=halo_recv.at[1],
            device_id={"space": space - 1}, device_id_type=MESH)

    degree = (ndate - 1) + 1 + jnp.where(space > 0, 1, 0) + jnp.where(space < nspace - 1, 1, 0)
    pl.semaphore_wait(barrier, degree)
    for r in list(range(3)) + list(range(ROWS - 3, ROWS)):
        for copy in loads(r):
            copy.wait()

    @pl.when(space < nspace - 1)
    def _():
        down().start()

    @pl.when(space > 0)
    def _():
        up().start()

    @pl.when(space == 0)
    def _():
        xin[0:3] = jnp.zeros((3, 2, 8, wide), F32)

    @pl.when(space == nspace - 1)
    def _():
        xin[ROWS + 3 : ROWS + 6] = jnp.zeros((3, 2, 8, wide), F32)

    def send(r):
        for k in range(1, ndate):
            peer = lax.rem(date + k, ndate)
            pltpu.make_async_remote_copy(
                src_ref=sendbuf.at[r, peer], dst_ref=got.at[r, date],
                send_sem=send_sem, recv_sem=recv_sem.at[r],
                device_id={"date": peer}, device_id_type=MESH).start()
        pltpu.make_async_copy(sendbuf.at[r, date], got.at[r, date], own_sem.at[r]).start()

    lanes = lax.broadcasted_iota(jnp.int32, (16, 128), 1)
    width = wide // ndate

    def spread(i):
        halves = []
        for h in range(2):
            tiles = [xin[i, p, :, b * width + h * 128 : b * width + (h + 1) * 128] for b in range(ndate) for p in range(2)]
            half_row = jnp.concatenate(tiles, axis=0).T
            yy[0, i, LEFT + h * 128 : LEFT + (h + 1) * 128] = half_row
            halves.append(half_row)
        before = pltpu.roll(halves[1][112:], 16, axis=1)
        after = pltpu.roll(halves[0][:16], 112, axis=1)
        yy[0, i, LEFT - 16 : LEFT] = jnp.where(lanes >= 16, before, 0.0)
        yy[0, i, LEFT + 256 : LEFT + 272] = jnp.where(lanes < 112, after, 0.0)
        for n in range(4):
            at = slice(LEFT - 16 + n * 72, LEFT - 16 + (n + 1) * 72)
            x = yy[0, i, at]
            yy[1, i, at] = x * x
        for q in range(2):
            for n in range(3):
                at = LEFT - 8 + n * 88
                four = (yy[q, i, at : at + 88] + yy[q, i, at + 1 : at + 89]) + (yy[q, i, at + 2 : at + 90] + yy[q, i, at + 3 : at + 91])
                a0[q, i, n * 88 : (n + 1) * 88] = four
            for n in range(4):
                at = 64 * n
                r7[q, i, at : at + 64] = a0[q, i, at + 8 : at + 72] + a0[q, i, at + 5 : at + 69] - yy[q, i, LEFT + at : LEFT + at + 64]

    def diagonals(rows):
        for n, r in enumerate(sorted(rows)):
            for q in range(2):
                for k in range(2):
                    side = -1 if k == 0 else 1
                    for m in range(3):
                        at = LEFT - 8 * k + 88 * m

                        def x(i, off):
                            return yy[q, i, at + off : at + off + 88]

                        if n == 0:
                            total = x(r, -3 * side)
                            for i in range(1, 7):
                                total = total + x(r + i, (i - 3) * side)
                        else:
                            total = dd[n - 1, q, k, at - side : at - side + 88] - x(r - 1, -4 * side) + x(r + 6, 3 * side)
                        dd[n, q, k, at : at + 88] = total

    def windows(rows, init):
        step = rows[1] - rows[0]

        def tile(t, carry):
            at = pl.multiple_of(t * 8, 8)
            here = pl.ds(at, 8)
            pairs, quads, state, cols = {}, {}, {}, {}

            def x(q, i, off):
                return yy[q, i, pl.ds(at + LEFT + off, 8), :]

            def row(q, i):
                return r7[q, i, here, :]

            def pair(q, i):
                if (q, i) not in pairs:
                    pairs[q, i] = row(q, i) + row(q, i + 1)
                return pairs[q, i]

            def quad(q, i):
                if (q, i) not in quads:
                    quads[q, i] = pair(q, i) + pair(q, i + 2)
                return quads[q, i]

            def start(q, r):
                total = [None] * 4
                for k in range(-3, 4):
                    i, m = r + 3 + k, abs(k)
                    four, ruof = a0[q, i, pl.ds(at + 8, 8), :], a0[q, i, pl.ds(at + 5, 8), :]
                    if m == 0:
                        parts = (four, four, ruof, ruof)
                    elif m == 1:
                        mid = x(q, i, 0)
                        parts = (four + x(q, i, -1), four - mid, ruof - mid, ruof + x(q, i, 1))
                    elif m == 2:
                        whole, low, high = row(q, i), x(q, i, -3), x(q, i, 3)
                        parts = (whole - low, high + x(q, i, 2), low + x(q, i, -2), whole - high)
                    else:
                        whole = row(q, i)
                        parts = (whole, x(q, i, 3), x(q, i, -3), whole)
                    if k < 0:
                        parts = (parts[1], parts[0], parts[3], parts[2])
                    total = [p if t is None else t + p for t, p in zip(total, parts)]
                return total

            for n, r in enumerate(rows):
                e = ey[n, here, :]
                b0 = (e & 1) > 0
                b1 = (e & 2) > 0
                b2 = e > 3
                for q in range(2):
                    slot = sorted(rows).index(r)
                    d1 = dd[slot, q, 0, pl.ds(at + LEFT, 8), :]
                    d2 = dd[slot, q, 1, pl.ds(at + LEFT, 8), :]
                    if n == 0 and init:
                        t1, t3, t5, t7 = start(q, r)
                        for k, value in enumerate((t1, t3 - d2, t5 - d1, t7)):
                            behind[q, k, here, :] = value
                        state[q] = (t1 - d1, t3, t5, t7 - d2)
                    else:
                        if n == 0:
                            state[q] = [(ahead if step > 0 else behind)[q, k, here, :] for k in range(4)]
                        t1, t3, t5, t7 = state[q]
                        if step > 0:
                            new, old = row(q, r + 6), row(q, r - 1)
                            t1, t7 = t1 + new, t7 + new
                            t3, t5 = t3 + d2 - old, t5 + d1 - old
                            state[q] = (t1 - d1, t3, t5, t7 - d2)
                        else:
                            new, old = row(q, r), row(q, r + 7)
                            t3, t5 = t3 + new, t5 + new
                            t1, t7 = t1 + d1 - old, t7 + d2 - old
                            state[q] = (t1, t3 - d2, t5 - d1, t7)
                    if n == 0:
                        both = []
                        for off in (8, 5):
                            total = a0[q, r, pl.ds(at + off, 8), :]
                            for i in range(1, 7):
                                total = total + a0[q, r + i, pl.ds(at + off, 8), :]
                            both.append(total)
                    else:
                        new, old = (r + 6, r - 1) if step > 0 else (r, r + 7)
                        both = [
                            total + a0[q, new, pl.ds(at + off, 8), :] - a0[q, old, pl.ds(at + off, 8), :]
                            for total, off in zip(cols[q], (8, 5))
                        ]
                    cols[q] = both
                    s02 = jnp.where(b1, both[0], quad(q, r + 3))
                    s46 = jnp.where(b1, both[1], quad(q, r))
                    s13 = jnp.where(b1, t3, t1)
                    s57 = jnp.where(b1, t7, t5)
                    ff[n, q, here, :] = jnp.where(b2, jnp.where(b0, s57, s46), jnp.where(b0, s13, s02))
            if step > 0:
                for q in range(2):
                    for k in range(4):
                        ahead[q, k, here, :] = state[q][k]
            return carry

        lax.fori_loop(0, 32, tile, 0)

    def group(rows, init=False):
        for n, r in enumerate(rows):
            for h in range(2):
                tiles = [ein[r, :, b * width + h * 128 : b * width + (h + 1) * 128] for b in range(ndate) for p in range(2)]
                ey[n, h * 128 : (h + 1) * 128] = jnp.concatenate(tiles, axis=0).T
        diagonals(rows)
        windows(rows, init)
        for n, r in enumerate(rows):
            for h in range(2):
                half_row = slice(h * 128, (h + 1) * 128)
                x = yy[0, r + 3, LEFT + h * 128 : LEFT + (h + 1) * 128]
                mean = ff[n, 0, half_row] * (1.0 / 28.0)
                sq_mean = mean * mean
                excess = jnp.maximum(ff[n, 1, half_row] * (1.0 / 28.0) - 1.25 * sq_mean, 0.0)
                under = excess + 0.3125 * sq_mean
                inv = pl.reciprocal(under, approx=True)
                inv = inv * (2.0 - under * inv)
                filtered = mean + excess * inv * (x - mean)
                level = (jnp.log(filtered) * LOG10E).T
                sendbuf[r, :, :, half_row] = level.astype(BF16).reshape(ndate, 16, 128)
            send(r)

    def spread_step(waits):
        def body(i, carry):
            if waits:
                @pl.when(jnp.logical_and(i >= 6, i < ROWS))
                def _():
                    for copy in loads(i - 3):
                        copy.wait()
            spread(i)
            return carry

        return body

    lax.fori_loop(3, 14, spread_step(True), 0)
    group([3, 4, 5, 6, 7], init=True)
    lax.fori_loop(14, ROWS + 3, spread_step(True), 0)
    group([8, 9, 10, 11, 12])

    @pl.when(space < nspace - 1)
    def _():
        up().wait_recv()

    lax.fori_loop(ROWS + 3, ROWS + 6, spread_step(False), 0)
    group([13, 14, 15])

    @pl.when(space > 0)
    def _():
        down().wait_recv()

    lax.fori_loop(0, 3, spread_step(False), 0)
    group([2, 1, 0])

    acc[...] = jnp.zeros(acc.shape, F32)
    ones = jnp.ones((wide // ndate, 128), BF16)

    def fit(r):
        pltpu.make_async_copy(got.at[r, 0 : ndate - 1], got.at[r, 0 : ndate - 1], recv_sem.at[r]).wait()
        pltpu.make_async_copy(sendbuf.at[r, date], got.at[r, date], own_sem.at[r]).wait()
        series = got[r].reshape(ndate * 16, wide // ndate)
        coeffs = lax.dot_general(series, basis_ref[...], (((0,), (0,)), ((), ())), preferred_element_type=F32)
        coeffs = coeffs.astype(BF16)
        out_ref[r] = coeffs
        acc[...] += jnp.dot(onehot[r], jnp.concatenate([coeffs, ones], axis=1), preferred_element_type=F32)

    def fit_step(m, carry):
        for k in range(4):
            n = 4 * m + k
            fit(jnp.where(n < ROWS - 3, n + 3, ROWS - 1 - n))
        return carry

    lax.fori_loop(0, ROWS // 4, fit_step, 0)

    high = date // half
    low = lax.rem(space, 2)
    copies = []
    for k in range(1, 4):
        far, near = k // 2, k % 2
        part = lax.rem(high + far, 2) * 2 + lax.rem(low + near, 2)
        copy = pltpu.make_async_remote_copy(
            src_ref=acc.at[pl.ds(pl.multiple_of(part * ROWS, ROWS), ROWS)], dst_ref=qgot.at[k - 1],
            send_sem=qsend.at[k - 1], recv_sem=qrecv.at[k - 1],
            device_id={"date": opposite if far else date, "space": mate if near else space}, device_id_type=MESH)
        copy.start()
        copies.append(copy)
    total = acc[pl.ds(pl.multiple_of((high * 2 + low) * ROWS, ROWS), ROWS), :]
    for k, copy in enumerate(copies):
        copy.wait_recv()
        total = total + qgot[k]
    means_ref[...] = total[:, :128] / jnp.maximum(total[:, 128:], 1.0)

    for copy in copies:
        copy.wait_send()
    pltpu.make_async_copy(sendbuf.at[:, 0 : ndate - 1], sendbuf.at[:, 0 : ndate - 1], send_sem).wait()

    @pl.when(space < nspace - 1)
    def _():
        down().wait_send()

    @pl.when(space > 0)
    def _():
        up().wait_send()


def solution(mesh):
    ndate, nspace = mesh.shape["date"], mesh.shape["space"]
    basis = basis_table(DATES, DATES // ndate, 2)

    def local(backscatter, edge_dirs, labels, parcel_slot):
        wide = backscatter.shape[3]
        cols = wide // ndate
        any_spec = pl.BlockSpec(memory_space=pl.ANY)
        vmem = pl.BlockSpec(memory_space=pltpu.VMEM)
        return pl.pallas_call(
            functools.partial(kernel, ndate, nspace, wide),
            out_shape=(
                jax.ShapeDtypeStruct((ROWS, cols, 128), BF16),
                jax.ShapeDtypeStruct((ROWS, 128), F32),
            ),
            in_specs=[any_spec, any_spec, vmem, vmem, vmem],
            out_specs=(vmem, vmem),
            scratch_shapes=[
                pltpu.VMEM((TALL, 2, 8, wide), F32),
                pltpu.VMEM((ROWS, 8, wide), jnp.int32),
                pltpu.VMEM((2, TALL, TALLER, 128), F32),
                pltpu.VMEM((2, TALL, 264, 128), F32),
                pltpu.VMEM((2, TALL, 256, 128), F32),
                pltpu.VMEM((GROUP, 2, 2, TALLER, 128), F32),
                pltpu.VMEM((GROUP, 2, 256, 128), F32),
                pltpu.VMEM((2, 4, 256, 128), F32),
                pltpu.VMEM((2, 4, 256, 128), F32),
                pltpu.VMEM((GROUP, 256, 128), jnp.int32),
                pltpu.VMEM((ROWS, ndate, 16, cols), BF16),
                pltpu.VMEM((ROWS, ndate, 16, cols), BF16),
                pltpu.VMEM((ROWS, 4 * ROWS, cols), BF16),
                pltpu.VMEM((4 * ROWS, 256), F32),
                pltpu.VMEM((3, ROWS, 256), F32),
                pltpu.SemaphoreType.DMA((ROWS, 3)),
                pltpu.SemaphoreType.DMA((2,)),
                pltpu.SemaphoreType.DMA((2,)),
                pltpu.SemaphoreType.DMA,
                pltpu.SemaphoreType.DMA((ROWS,)),
                pltpu.SemaphoreType.DMA((ROWS,)),
                pltpu.SemaphoreType.DMA((3,)),
                pltpu.SemaphoreType.DMA((3,)),
            ],
            compiler_params=pltpu.CompilerParams(
                collective_id=0, has_side_effects=True, vmem_limit_bytes=56 * 1024 * 1024
            ),
        )(backscatter, edge_dirs, labels, parcel_slot.reshape(-1, 128), jnp.asarray(basis))

    return jax.shard_map(
        local,
        mesh=mesh,
        in_specs=(P("date", None, "space", None), P("date", "space", None), P("space", "date"), P()),
        out_specs=(P("space", "date", None), P(("date", "space"), None)),
        check_vma=False,
    )
```

```python
import functools

import jax
import jax.numpy as jnp
import ml_dtypes
import numpy as np
from jax import lax
from jax.experimental import pallas as pl
from jax.experimental.pallas import tpu as pltpu
from jax.sharding import PartitionSpec as P

MESH = pl.DeviceIdType.MESH
F32 = jnp.float32
BF16 = jnp.bfloat16
DATES = 64
ROWS = 16
TALL = ROWS + 6
GROUP = 4
LATE = (10, 11, 12, 13, 14, 15, 2, 1, 0)
LOG10E = 0.4342944819032518
LEFT = 24
TALLER = LEFT + 256 + 24


def basis_table(dates, group, pols):
    times = np.arange(dates, dtype=np.float32)[:, None]
    index = np.arange(dates, dtype=np.float32)[None, :]
    half = dates // 2
    scale = np.sqrt(np.float32(2.0 / dates))
    cosine = np.cos(np.float32(2.0 * np.pi) * index * times / np.float32(dates))
    sine = np.sin(np.float32(2.0 * np.pi) * (index - half) * times / np.float32(dates))
    table = (np.where(index <= half, cosine, sine) * scale).astype(np.float32)
    wide = np.zeros((dates // group, pols, group, pols, dates), np.float32)
    for p in range(pols):
        wide[:, p, :, p, :] = table.reshape(dates // group, group, dates)
    return wide.reshape(dates * pols, pols * dates).astype(ml_dtypes.bfloat16)


def kernel(
    ndate, nspace, wide,
    x_hbm, e_hbm, labels_hbm, slot_hbm, basis_hbm,
    out_ref, means_ref,
    xin, ein, yy, a0, r7, dd, ff, ahead, behind, ey, sendbuf, got, onehot, acc, qgot, labels_ref, slot_ref, basis_ref,
    in_sem, small_sem, halo_send, halo_recv, send_sem, recv_sem, own_sem, qsend, qrecv,
):
    date = lax.axis_index("date")
    space = lax.axis_index("space")
    half = ndate // 2

    order = list(range(3)) + list(range(ROWS - 3, ROWS)) + list(range(3, ROWS - 3))

    def loads(r):
        for p in range(2):
            yield pltpu.make_async_copy(x_hbm.at[:, p, r, :], xin.at[r + 3, p], in_sem.at[r, p])
        yield pltpu.make_async_copy(e_hbm.at[:, r, :], ein.at[r], in_sem.at[r, 2])

    small = [
        pltpu.make_async_copy(source, target, small_sem.at[n])
        for n, (source, target) in enumerate(
            ((slot_hbm, slot_ref), (labels_hbm, labels_ref), (basis_hbm, basis_ref)))
    ]
    for copy in small:
        copy.start()
    for r in order:
        for copy in loads(r):
            copy.start()

    barrier = pltpu.get_barrier_semaphore()
    for k in range(1, ndate):
        pl.semaphore_signal(barrier, inc=1, device_id={"date": lax.rem(date + k, ndate)}, device_id_type=MESH)
    mate = space + 1 - 2 * lax.rem(space, 2)
    opposite = lax.rem(date + half, ndate)
    pl.semaphore_signal(barrier, inc=1, device_id={"date": opposite, "space": mate}, device_id_type=MESH)

    @pl.when(space > 0)
    def _():
        pl.semaphore_signal(barrier, inc=1, device_id={"space": space - 1}, device_id_type=MESH)

    @pl.when(space < nspace - 1)
    def _():
        pl.semaphore_signal(barrier, inc=1, device_id={"space": space + 1}, device_id_type=MESH)

    for copy in small:
        copy.wait()

    base_date = lax.rem(date, half)
    base_space = space - lax.rem(space, 2)
    parts = []
    for u in range(4):
        owner = (base_date + (u // 2) * half) * nspace + base_space + u % 2
        parts.append(lax.broadcasted_iota(jnp.int32, (ROWS, 128), 0) + owner * ROWS)
    ids = jnp.concatenate(parts, axis=0)
    lane = lax.broadcasted_iota(jnp.int32, (4 * ROWS, 128), 1).astype(F32)
    total = jnp.zeros((4 * ROWS, 128), F32)
    for g in range(slot_ref.shape[0]):
        total = total + jnp.where(ids == slot_ref[g : g + 1, :], lane + float(128 * g), 0.0)
    parcel_of = jnp.sum(total, axis=1, keepdims=True).astype(jnp.int32)
    for r in range(ROWS):
        onehot[r] = jnp.where(parcel_of == labels_ref[r : r + 1, :], 1.0, 0.0).astype(BF16)

    present = onehot[0].astype(F32)
    for r in range(1, ROWS):
        present = present + onehot[r].astype(F32)
    acc[:, :128] = jnp.zeros((4 * ROWS, 128), F32)
    acc[:, 128:] = jnp.broadcast_to(jnp.sum(present, axis=1, keepdims=True), (4 * ROWS, 128))

    def down():
        return pltpu.make_async_remote_copy(
            src_ref=xin.at[ROWS : ROWS + 3], dst_ref=xin.at[0:3],
            send_sem=halo_send.at[0], recv_sem=halo_recv.at[0],
            device_id={"space": space + 1}, device_id_type=MESH)

    def up():
        return pltpu.make_async_remote_copy(
            src_ref=xin.at[3:6], dst_ref=xin.at[ROWS + 3 : ROWS + 6],
            send_sem=halo_send.at[1], recv_sem=halo_recv.at[1],
            device_id={"space": space - 1}, device_id_type=MESH)

    degree = (ndate - 1) + 1 + jnp.where(space > 0, 1, 0) + jnp.where(space < nspace - 1, 1, 0)
    pl.semaphore_wait(barrier, degree)
    for r in list(range(3)) + list(range(ROWS - 3, ROWS)):
        for copy in loads(r):
            copy.wait()

    @pl.when(space < nspace - 1)
    def _():
        down().start()

    @pl.when(space > 0)
    def _():
        up().start()

    @pl.when(space == 0)
    def _():
        xin[0:3] = jnp.zeros((3, 2, 8, wide), F32)

    @pl.when(space == nspace - 1)
    def _():
        xin[ROWS + 3 : ROWS + 6] = jnp.zeros((3, 2, 8, wide), F32)

    def send(r):
        for k in range(1, ndate):
            peer = lax.rem(date + k, ndate)
            pltpu.make_async_remote_copy(
                src_ref=sendbuf.at[r, peer], dst_ref=got.at[r, date],
                send_sem=send_sem, recv_sem=recv_sem.at[r],
                device_id={"date": peer}, device_id_type=MESH).start()
        pltpu.make_async_copy(sendbuf.at[r, date], got.at[r, date], own_sem.at[r]).start()

    lanes = lax.broadcasted_iota(jnp.int32, (16, 128), 1)
    width = wide // ndate

    def spread(i):
        halves = []
        for h in range(2):
            tiles = [xin[i, p, :, b * width + h * 128 : b * width + (h + 1) * 128] for b in range(ndate) for p in range(2)]
            half_row = jnp.concatenate(tiles, axis=0).T
            yy[0, i, LEFT + h * 128 : LEFT + (h + 1) * 128] = half_row
            halves.append(half_row)
        before = pltpu.roll(halves[1][112:], 16, axis=1)
        after = pltpu.roll(halves[0][:16], 112, axis=1)
        yy[0, i, LEFT - 16 : LEFT] = jnp.where(lanes >= 16, before, 0.0)
        yy[0, i, LEFT + 256 : LEFT + 272] = jnp.where(lanes < 112, after, 0.0)
        for at, size in ((LEFT - 16, 8), (LEFT + 256, 16)):
            x = yy[0, i, at : at + size]
            yy[1, i, at : at + size] = x * x
        for n in range(4):
            start, size = (0, 72) if n == 0 else (8 + 64 * n, 64)
            at = LEFT - 8 + start
            shifted = [yy[0, i, at + k : at + k + size] for k in range(4)]
            for q in range(2):
                if q:
                    shifted = [x * x for x in shifted]
                    yy[1, i, at : at + size] = shifted[0]
                four = (shifted[0] + shifted[1]) + (shifted[2] + shifted[3])
                a0[q, i, start : start + size] = four
                skip = 8 if n == 0 else 0
                r7[q, i, 64 * n : 64 * n + 64] = (
                    four[skip:] + a0[q, i, start + skip - 3 : start + size - 3] - shifted[0][skip:]
                )

    def diagonals(rows):
        for n, r in enumerate(sorted(rows)):
            for q in range(2):
                for k in range(2):
                    side = -1 if k == 0 else 1
                    for m in range(3):
                        at = LEFT - 8 * k + 88 * m

                        def x(i, off):
                            return yy[q, i, at + off : at + off + 88]

                        if n == 0:
                            total = x(r, -3 * side)
                            for i in range(1, 7):
                                total = total + x(r + i, (i - 3) * side)
                        else:
                            total = dd[n - 1, q, k, at - side : at - side + 88] - x(r - 1, -4 * side) + x(r + 6, 3 * side)
                        dd[n, q, k, at : at + 88] = total

    def windows(rows, init):
        step = rows[1] - rows[0]

        def tile(t, carry):
            at = pl.multiple_of(t * 8, 8)
            here = pl.ds(at, 8)
            pairs, quads, state, cols = {}, {}, {}, {}

            def x(q, i, off):
                return yy[q, i, pl.ds(at + LEFT + off, 8), :]

            def row(q, i):
                return r7[q, i, here, :]

            def pair(q, i):
                if (q, i) not in pairs:
                    pairs[q, i] = row(q, i) + row(q, i + 1)
                return pairs[q, i]

            def quad(q, i):
                if (q, i) not in quads:
                    quads[q, i] = pair(q, i) + pair(q, i + 2)
                return quads[q, i]

            def start(q, r):
                total = [None] * 4
                for k in range(-3, 4):
                    i, m = r + 3 + k, abs(k)
                    four, ruof = a0[q, i, pl.ds(at + 8, 8), :], a0[q, i, pl.ds(at + 5, 8), :]
                    if m == 0:
                        parts = (four, four, ruof, ruof)
                    elif m == 1:
                        mid = x(q, i, 0)
                        parts = (four + x(q, i, -1), four - mid, ruof - mid, ruof + x(q, i, 1))
                    elif m == 2:
                        whole, low, high = row(q, i), x(q, i, -3), x(q, i, 3)
                        parts = (whole - low, high + x(q, i, 2), low + x(q, i, -2), whole - high)
                    else:
                        whole = row(q, i)
                        parts = (whole, x(q, i, 3), x(q, i, -3), whole)
                    if k < 0:
                        parts = (parts[1], parts[0], parts[3], parts[2])
                    total = [p if t is None else t + p for t, p in zip(total, parts)]
                return total

            for n, r in enumerate(rows):
                e = ey[n, here, :]
                b0 = (e & 1) > 0
                b1 = (e & 2) > 0
                b2 = e > 3
                for q in range(2):
                    slot = sorted(rows).index(r)
                    d1 = dd[slot, q, 0, pl.ds(at + LEFT, 8), :]
                    d2 = dd[slot, q, 1, pl.ds(at + LEFT, 8), :]
                    if n == 0 and init:
                        t1, t3, t5, t7 = start(q, r)
                        for k, value in enumerate((t1, t3 - d2, t5 - d1, t7)):
                            behind[q, k, here, :] = value
                        state[q] = (t1 - d1, t3, t5, t7 - d2)
                    else:
                        if n == 0:
                            state[q] = [(ahead if step > 0 else behind)[q, k, here, :] for k in range(4)]
                        t1, t3, t5, t7 = state[q]
                        if step > 0:
                            new, old = row(q, r + 6), row(q, r - 1)
                            t1, t7 = t1 + new, t7 + new
                            t3, t5 = t3 + d2 - old, t5 + d1 - old
                            state[q] = (t1 - d1, t3, t5, t7 - d2)
                        else:
                            new, old = row(q, r), row(q, r + 7)
                            t3, t5 = t3 + new, t5 + new
                            t1, t7 = t1 + d1 - old, t7 + d2 - old
                            state[q] = (t1, t3 - d2, t5 - d1, t7)
                    if n == 0:
                        both = []
                        for off in (8, 5):
                            total = a0[q, r, pl.ds(at + off, 8), :]
                            for i in range(1, 7):
                                total = total + a0[q, r + i, pl.ds(at + off, 8), :]
                            both.append(total)
                    else:
                        new, old = (r + 6, r - 1) if step > 0 else (r, r + 7)
                        both = [
                            total + a0[q, new, pl.ds(at + off, 8), :] - a0[q, old, pl.ds(at + off, 8), :]
                            for total, off in zip(cols[q], (8, 5))
                        ]
                    cols[q] = both
                    s02 = jnp.where(b1, both[0], quad(q, r + 3))
                    s46 = jnp.where(b1, both[1], quad(q, r))
                    s13 = jnp.where(b1, t3, t1)
                    s57 = jnp.where(b1, t7, t5)
                    ff[n, q, here, :] = jnp.where(b2, jnp.where(b0, s57, s46), jnp.where(b0, s13, s02))
            if step > 0:
                for q in range(2):
                    for k in range(4):
                        ahead[q, k, here, :] = state[q][k]
            return carry

        lax.fori_loop(0, 16, lambda t, carry: tile(2 * t + 1, tile(2 * t, carry)), 0)

    def group(rows, init=False):
        for n, r in enumerate(rows):
            for h in range(2):
                tiles = [ein[r, :, b * width + h * 128 : b * width + (h + 1) * 128] for b in range(ndate) for p in range(2)]
                ey[n, h * 128 : (h + 1) * 128] = jnp.concatenate(tiles, axis=0).T
        diagonals(rows)
        windows(rows, init)
        for n, r in enumerate(rows):
            for h in range(2):
                half_row = slice(h * 128, (h + 1) * 128)
                x = yy[0, r + 3, LEFT + h * 128 : LEFT + (h + 1) * 128]
                mean = ff[n, 0, half_row] * (1.0 / 28.0)
                sq_mean = mean * mean
                excess = jnp.maximum(ff[n, 1, half_row] * (1.0 / 28.0) - 1.25 * sq_mean, 0.0)
                under = excess + 0.3125 * sq_mean
                inv = pl.reciprocal(under, approx=True)
                filtered = mean + excess * inv * (x - mean)
                level = (jnp.log(filtered) * LOG10E).T
                sendbuf[r, :, :, half_row] = level.astype(BF16).reshape(ndate, 16, 128)
            send(r)

    def spread_step(waits):
        def body(i, carry):
            if waits:
                @pl.when(jnp.logical_and(i >= 6, i < ROWS))
                def _():
                    for copy in loads(i - 3):
                        copy.wait()
            spread(i)
            return carry

        return body

    def fit(r):
        series = got[r].reshape(ndate * 16, width)
        coeffs = lax.dot_general(series, basis_ref[...], (((0,), (0,)), ((), ())), preferred_element_type=F32)
        out_ref[r] = coeffs.astype(BF16)

    def take(rows):
        for r in rows:
            pltpu.make_async_copy(got.at[r, 0 : ndate - 1], got.at[r, 0 : ndate - 1], recv_sem.at[r]).wait()
            pltpu.make_async_copy(sendbuf.at[r, date], got.at[r, date], own_sem.at[r]).wait()
        total = acc[:, :128]
        for r in rows:
            series = got[r].reshape(ndate * 16, width)
            total = total + lax.dot_general(onehot[r], series, (((1,), (1,)), ((), ())), preferred_element_type=F32)
        acc[:, :128] = total
        for r in rows:
            if r not in LATE:
                fit(r)

    lax.fori_loop(3, 12, spread_step(True), 0)
    group([3, 4, 5], init=True)
    lax.fori_loop(12, 16, spread_step(True), 0)
    group([6, 7, 8, 9])
    lax.fori_loop(16, ROWS + 3, spread_step(True), 0)
    group([10, 11, 12])
    take(range(3, 6))

    @pl.when(space < nspace - 1)
    def _():
        up().wait_recv()

    lax.fori_loop(ROWS + 3, ROWS + 6, spread_step(False), 0)
    group([13, 14, 15])
    take(range(6, 9))

    @pl.when(space > 0)
    def _():
        down().wait_recv()

    lax.fori_loop(0, 3, spread_step(False), 0)
    group([2, 1, 0])
    take(range(9, ROWS))
    take(range(3))

    high = date // half
    low = lax.rem(space, 2)
    copies = []
    for k in range(1, 4):
        far, near = k // 2, k % 2
        part = lax.rem(high + far, 2) * 2 + lax.rem(low + near, 2)
        copy = pltpu.make_async_remote_copy(
            src_ref=acc.at[pl.ds(pl.multiple_of(part * ROWS, ROWS), ROWS)], dst_ref=qgot.at[k - 1],
            send_sem=qsend.at[k - 1], recv_sem=qrecv.at[k - 1],
            device_id={"date": opposite if far else date, "space": mate if near else space}, device_id_type=MESH)
        copy.start()
        copies.append(copy)

    for r in LATE:
        fit(r)
    total = acc[pl.ds(pl.multiple_of((high * 2 + low) * ROWS, ROWS), ROWS), :]
    for k, copy in enumerate(copies):
        copy.wait_recv()
        total = total + qgot[k]
    sums, counts = total[:, :128], total[:, 128:]
    coarse = sums.astype(BF16)
    fine = (sums - coarse.astype(F32)).astype(BF16)
    sums = jnp.dot(coarse, basis_ref[...], preferred_element_type=F32) + jnp.dot(fine, basis_ref[...], preferred_element_type=F32)
    means_ref[...] = sums / jnp.maximum(counts, 1.0)

    for copy in copies:
        copy.wait_send()
    pltpu.make_async_copy(sendbuf.at[:, 0 : ndate - 1], sendbuf.at[:, 0 : ndate - 1], send_sem).wait()

    @pl.when(space < nspace - 1)
    def _():
        down().wait_send()

    @pl.when(space > 0)
    def _():
        up().wait_send()


def solution(mesh):
    ndate, nspace = mesh.shape["date"], mesh.shape["space"]
    basis = basis_table(DATES, DATES // ndate, 2)

    def local(backscatter, edge_dirs, labels, parcel_slot):
        wide = backscatter.shape[3]
        cols = wide // ndate
        hbm = pl.BlockSpec(memory_space=pltpu.HBM)
        vmem = pl.BlockSpec(memory_space=pltpu.VMEM)
        return pl.pallas_call(
            functools.partial(kernel, ndate, nspace, wide),
            out_shape=(
                jax.ShapeDtypeStruct((ROWS, cols, 128), BF16),
                jax.ShapeDtypeStruct((ROWS, 128), F32),
            ),
            in_specs=[hbm] * 5,
            out_specs=(vmem, vmem),
            scratch_shapes=[
                pltpu.VMEM((TALL, 2, 8, wide), F32),
                pltpu.VMEM((ROWS, 8, wide), jnp.int32),
                pltpu.VMEM((2, TALL, TALLER, 128), F32),
                pltpu.VMEM((2, TALL, 264, 128), F32),
                pltpu.VMEM((2, TALL, 256, 128), F32),
                pltpu.VMEM((GROUP, 2, 2, TALLER, 128), F32),
                pltpu.VMEM((GROUP, 2, 256, 128), F32),
                pltpu.VMEM((2, 4, 256, 128), F32),
                pltpu.VMEM((2, 4, 256, 128), F32),
                pltpu.VMEM((GROUP, 256, 128), jnp.int32),
                pltpu.VMEM((ROWS, ndate, 16, cols), BF16),
                pltpu.VMEM((ROWS, ndate, 16, cols), BF16),
                pltpu.VMEM((ROWS, 4 * ROWS, cols), BF16),
                pltpu.VMEM((4 * ROWS, 256), F32),
                pltpu.VMEM((3, ROWS, 256), F32),
                pltpu.VMEM(labels.shape, jnp.int32),
                pltpu.VMEM((parcel_slot.shape[0] // 128, 128), jnp.int32),
                pltpu.VMEM(basis.shape, BF16),
                pltpu.SemaphoreType.DMA((ROWS, 3)),
                pltpu.SemaphoreType.DMA((3,)),
                pltpu.SemaphoreType.DMA((2,)),
                pltpu.SemaphoreType.DMA((2,)),
                pltpu.SemaphoreType.DMA,
                pltpu.SemaphoreType.DMA((ROWS,)),
                pltpu.SemaphoreType.DMA((ROWS,)),
                pltpu.SemaphoreType.DMA((3,)),
                pltpu.SemaphoreType.DMA((3,)),
            ],
            compiler_params=pltpu.CompilerParams(
                collective_id=0, has_side_effects=True, vmem_limit_bytes=52 * 1024 * 1024
            ),
        )(*[
            pltpu.with_memory_space_constraint(v, pltpu.HBM)
            for v in (backscatter, edge_dirs, labels, parcel_slot.reshape(-1, 128), jnp.asarray(basis))
        ])

    return jax.shard_map(
        local,
        mesh=mesh,
        in_specs=(P("date", None, "space", None), P("date", "space", None), P("space", "date"), P()),
        out_specs=(P("space", "date", None), P(("date", "space"), None)),
        check_vma=False,
    )
```

```python
import functools

import jax
import jax.numpy as jnp
import ml_dtypes
import numpy as np
from jax import lax
from jax.experimental import pallas as pl
from jax.experimental.pallas import tpu as pltpu
from jax.sharding import PartitionSpec as P

MESH = pl.DeviceIdType.MESH
F32 = jnp.float32
BF16 = jnp.bfloat16
DATES = 64
ROWS = 16
TALL = ROWS + 6
GROUP = 4
LOG10E = 0.4342944819032518
STEPS = 65535.0
MIDDLE = 32768.0
LEFT = 24
TALLER = LEFT + 256 + 24


def basis_table(dates, group, pols):
    times = np.arange(dates, dtype=np.float32)[:, None]
    index = np.arange(dates, dtype=np.float32)[None, :]
    half = dates // 2
    scale = np.sqrt(np.float32(2.0 / dates))
    cosine = np.cos(np.float32(2.0 * np.pi) * index * times / np.float32(dates))
    sine = np.sin(np.float32(2.0 * np.pi) * (index - half) * times / np.float32(dates))
    table = (np.where(index <= half, cosine, sine) * scale).astype(np.float32)
    wide = np.zeros((dates // group, pols, group, pols, dates), np.float32)
    for p in range(pols):
        wide[:, p, :, p, :] = table.reshape(dates // group, group, dates)
    return wide.reshape(dates * pols, pols * dates).astype(ml_dtypes.bfloat16)


def kernel(
    ndate, nspace, wide,
    x_hbm, e_hbm, labels_hbm, slot_hbm,
    got, total_ref,
    xin, ein, yy, a0, r7, dd, ff, ahead, behind, ey, sendbuf, onehot, acc, qgot, labels_ref, slot_ref, edge_out, edge_in,
    in_sem, small_sem, halo_send, halo_recv, send_sem, recv_sem, own_sem, qsend, qrecv,
):
    date = lax.axis_index("date")
    space = lax.axis_index("space")
    half = ndate // 2

    order = list(range(9)) + list(range(ROWS - 3, ROWS)) + list(range(9, ROWS - 3))

    def loads(r):
        for p in range(2):
            yield pltpu.make_async_copy(x_hbm.at[:, p, r, :], xin.at[r + 3, p], in_sem.at[r, p])
        yield pltpu.make_async_copy(e_hbm.at[:, r, :], ein.at[r], in_sem.at[r, 2])

    small = [
        pltpu.make_async_copy(source, target, small_sem.at[n])
        for n, (source, target) in enumerate(
            ((slot_hbm, slot_ref), (labels_hbm, labels_ref)))
    ]
    for copy in small:
        copy.start()
    for r in order:
        for copy in loads(r):
            copy.start()

    barrier = pltpu.get_barrier_semaphore()
    for k in range(1, ndate):
        pl.semaphore_signal(barrier, inc=1, device_id={"date": lax.rem(date + k, ndate)}, device_id_type=MESH)
    mate = space + 1 - 2 * lax.rem(space, 2)
    opposite = lax.rem(date + half, ndate)
    pl.semaphore_signal(barrier, inc=1, device_id={"date": opposite, "space": mate}, device_id_type=MESH)

    @pl.when(space > 0)
    def _():
        pl.semaphore_signal(barrier, inc=1, device_id={"space": space - 1}, device_id_type=MESH)

    @pl.when(space < nspace - 1)
    def _():
        pl.semaphore_signal(barrier, inc=1, device_id={"space": space + 1}, device_id_type=MESH)

    for copy in small:
        copy.wait()

    base_date = lax.rem(date, half)
    base_space = space - lax.rem(space, 2)
    parts = []
    for u in range(4):
        owner = (base_date + (u // 2) * half) * nspace + base_space + u % 2
        parts.append(lax.broadcasted_iota(jnp.int32, (ROWS, 128), 0) + owner * ROWS)
    ids = jnp.concatenate(parts, axis=0)
    lane = lax.broadcasted_iota(jnp.int32, (4 * ROWS, 128), 1).astype(F32)
    total = jnp.zeros((4 * ROWS, 128), F32)
    for g in range(slot_ref.shape[0]):
        total = total + jnp.where(ids == slot_ref[g : g + 1, :], lane + float(128 * g), 0.0)
    parcel_of = jnp.sum(total, axis=1, keepdims=True).astype(jnp.int32)
    for r in range(ROWS):
        onehot[r] = jnp.where(parcel_of == labels_ref[r : r + 1, :], 1.0, 0.0).astype(BF16)

    present = onehot[0].astype(F32)
    for r in range(1, ROWS):
        present = present + onehot[r].astype(F32)
    acc[:, :128] = jnp.zeros((4 * ROWS, 128), F32)
    acc[:, 128:] = jnp.broadcast_to(jnp.sum(present, axis=1, keepdims=True), (4 * ROWS, 128))

    def down():
        return pltpu.make_async_remote_copy(
            src_ref=edge_out.at[1], dst_ref=edge_in.at[0],
            send_sem=halo_send.at[0], recv_sem=halo_recv.at[0],
            device_id={"space": space + 1}, device_id_type=MESH)

    def up():
        return pltpu.make_async_remote_copy(
            src_ref=edge_out.at[0], dst_ref=edge_in.at[1],
            send_sem=halo_send.at[1], recv_sem=halo_recv.at[1],
            device_id={"space": space - 1}, device_id_type=MESH)

    def pack(side, first):
        for k in range(3):
            x = xin[first + k].reshape(16, wide)
            edge_out[side, k] = ((x * STEPS + 0.5).astype(jnp.int32) - 32768).astype(jnp.int16)

    def unpack(side, first):
        for k in range(3):
            x = (edge_in[side, k].astype(jnp.int32).astype(F32) + MIDDLE) * (1.0 / STEPS)
            xin[first + k] = x.reshape(2, 8, wide)

    def halo_out():
        for r in range(ROWS - 3, ROWS):
            for copy in loads(r):
                copy.wait()
        pack(0, 3)
        pack(1, ROWS)

        @pl.when(space < nspace - 1)
        def _():
            down().start()

        @pl.when(space > 0)
        def _():
            up().start()

    degree = (ndate - 1) + 1 + jnp.where(space > 0, 1, 0) + jnp.where(space < nspace - 1, 1, 0)

    @pl.when(space == 0)
    def _():
        xin[0:3] = jnp.zeros((3, 2, 8, wide), F32)

    @pl.when(space == nspace - 1)
    def _():
        xin[ROWS + 3 : ROWS + 6] = jnp.zeros((3, 2, 8, wide), F32)

    def send(r):
        for k in range(1, ndate):
            peer = lax.rem(date + k, ndate)
            pltpu.make_async_remote_copy(
                src_ref=sendbuf.at[r, peer], dst_ref=got.at[r, date],
                send_sem=send_sem, recv_sem=recv_sem.at[r],
                device_id={"date": peer}, device_id_type=MESH).start()
        pltpu.make_async_copy(sendbuf.at[r, date], got.at[r, date], own_sem.at[r]).start()

    lanes = lax.broadcasted_iota(jnp.int32, (16, 128), 1)
    width = wide // ndate

    def spread(i):
        halves = []
        for h in range(2):
            tiles = [xin[i, p, :, b * width + h * 128 : b * width + (h + 1) * 128] for b in range(ndate) for p in range(2)]
            half_row = jnp.concatenate(tiles, axis=0).T
            yy[0, i, LEFT + h * 128 : LEFT + (h + 1) * 128] = half_row
            halves.append(half_row)
        before = pltpu.roll(halves[1][112:], 16, axis=1)
        after = pltpu.roll(halves[0][:16], 112, axis=1)
        yy[0, i, LEFT - 16 : LEFT] = jnp.where(lanes >= 16, before, 0.0)
        yy[0, i, LEFT + 256 : LEFT + 272] = jnp.where(lanes < 112, after, 0.0)
        for at, size in ((LEFT - 16, 8), (LEFT + 256, 16)):
            x = yy[0, i, at : at + size]
            yy[1, i, at : at + size] = x * x
        for n in range(4):
            start, size = (0, 72) if n == 0 else (8 + 64 * n, 64)
            at = LEFT - 8 + start
            shifted = [yy[0, i, at + k : at + k + size] for k in range(4)]
            for q in range(2):
                if q:
                    shifted = [x * x for x in shifted]
                    yy[1, i, at : at + size] = shifted[0]
                four = (shifted[0] + shifted[1]) + (shifted[2] + shifted[3])
                a0[q, i, start : start + size] = four
                skip = 8 if n == 0 else 0
                r7[q, i, 64 * n : 64 * n + 64] = (
                    four[skip:] + a0[q, i, start + skip - 3 : start + size - 3] - shifted[0][skip:]
                )

    def diagonals(rows):
        for n, r in enumerate(sorted(rows)):
            for q in range(2):
                for k in range(2):
                    side = -1 if k == 0 else 1
                    for m in range(3):
                        at = LEFT - 8 * k + 88 * m

                        def x(i, off):
                            return yy[q, i, at + off : at + off + 88]

                        if n == 0:
                            total = x(r, -3 * side)
                            for i in range(1, 7):
                                total = total + x(r + i, (i - 3) * side)
                        else:
                            total = dd[n - 1, q, k, at - side : at - side + 88] - x(r - 1, -4 * side) + x(r + 6, 3 * side)
                        dd[n, q, k, at : at + 88] = total

    def windows(rows, init):
        step = rows[1] - rows[0]

        def tile(t, carry):
            at = pl.multiple_of(t * 8, 8)
            here = pl.ds(at, 8)
            pairs, quads, state, cols = {}, {}, {}, {}

            def x(q, i, off):
                return yy[q, i, pl.ds(at + LEFT + off, 8), :]

            def row(q, i):
                return r7[q, i, here, :]

            def pair(q, i):
                if (q, i) not in pairs:
                    pairs[q, i] = row(q, i) + row(q, i + 1)
                return pairs[q, i]

            def quad(q, i):
                if (q, i) not in quads:
                    quads[q, i] = pair(q, i) + pair(q, i + 2)
                return quads[q, i]

            def start(q, r):
                total = [None] * 4
                for k in range(-3, 4):
                    i, m = r + 3 + k, abs(k)
                    four, ruof = a0[q, i, pl.ds(at + 8, 8), :], a0[q, i, pl.ds(at + 5, 8), :]
                    if m == 0:
                        parts = (four, four, ruof, ruof)
                    elif m == 1:
                        mid = x(q, i, 0)
                        parts = (four + x(q, i, -1), four - mid, ruof - mid, ruof + x(q, i, 1))
                    elif m == 2:
                        whole, low, high = row(q, i), x(q, i, -3), x(q, i, 3)
                        parts = (whole - low, high + x(q, i, 2), low + x(q, i, -2), whole - high)
                    else:
                        whole = row(q, i)
                        parts = (whole, x(q, i, 3), x(q, i, -3), whole)
                    if k < 0:
                        parts = (parts[1], parts[0], parts[3], parts[2])
                    total = [p if t is None else t + p for t, p in zip(total, parts)]
                return total

            for n, r in enumerate(rows):
                e = ey[n, here, :]
                b0 = (e & 1) > 0
                b1 = (e & 2) > 0
                b2 = e > 3
                for q in range(2):
                    slot = sorted(rows).index(r)
                    d1 = dd[slot, q, 0, pl.ds(at + LEFT, 8), :]
                    d2 = dd[slot, q, 1, pl.ds(at + LEFT, 8), :]
                    if n == 0 and init:
                        t1, t3, t5, t7 = start(q, r)
                        for k, value in enumerate((t1, t3 - d2, t5 - d1, t7)):
                            behind[q, k, here, :] = value
                        state[q] = (t1 - d1, t3, t5, t7 - d2)
                    else:
                        if n == 0:
                            state[q] = [(ahead if step > 0 else behind)[q, k, here, :] for k in range(4)]
                        t1, t3, t5, t7 = state[q]
                        if step > 0:
                            new, old = row(q, r + 6), row(q, r - 1)
                            t1, t7 = t1 + new, t7 + new
                            t3, t5 = t3 + d2 - old, t5 + d1 - old
                            state[q] = (t1 - d1, t3, t5, t7 - d2)
                        else:
                            new, old = row(q, r), row(q, r + 7)
                            t3, t5 = t3 + new, t5 + new
                            t1, t7 = t1 + d1 - old, t7 + d2 - old
                            state[q] = (t1, t3 - d2, t5 - d1, t7)
                    if n == 0:
                        both = []
                        for off in (8, 5):
                            total = a0[q, r, pl.ds(at + off, 8), :]
                            for i in range(1, 7):
                                total = total + a0[q, r + i, pl.ds(at + off, 8), :]
                            both.append(total)
                    else:
                        new, old = (r + 6, r - 1) if step > 0 else (r, r + 7)
                        both = [
                            total + a0[q, new, pl.ds(at + off, 8), :] - a0[q, old, pl.ds(at + off, 8), :]
                            for total, off in zip(cols[q], (8, 5))
                        ]
                    cols[q] = both
                    s02 = jnp.where(b1, both[0], quad(q, r + 3))
                    s46 = jnp.where(b1, both[1], quad(q, r))
                    s13 = jnp.where(b1, t3, t1)
                    s57 = jnp.where(b1, t7, t5)
                    ff[n, q, here, :] = jnp.where(b2, jnp.where(b0, s57, s46), jnp.where(b0, s13, s02))
            if step > 0:
                for q in range(2):
                    for k in range(4):
                        ahead[q, k, here, :] = state[q][k]
            return carry

        lax.fori_loop(0, 16, lambda t, carry: tile(2 * t + 1, tile(2 * t, carry)), 0)

    def group(rows, init=False):
        for n, r in enumerate(rows):
            for h in range(2):
                tiles = [ein[r, :, b * width + h * 128 : b * width + (h + 1) * 128] for b in range(ndate) for p in range(2)]
                ey[n, h * 128 : (h + 1) * 128] = jnp.concatenate(tiles, axis=0).T
        diagonals(rows)
        windows(rows, init)
        for n, r in enumerate(rows):
            for h in range(2):
                half_row = slice(h * 128, (h + 1) * 128)
                x = yy[0, r + 3, LEFT + h * 128 : LEFT + (h + 1) * 128]
                mean = ff[n, 0, half_row] * (1.0 / 28.0)
                sq_mean = mean * mean
                excess = jnp.maximum(ff[n, 1, half_row] * (1.0 / 28.0) - 1.25 * sq_mean, 0.0)
                under = excess + 0.3125 * sq_mean
                inv = pl.reciprocal(under, approx=True)
                filtered = mean + excess * inv * (x - mean)
                level = (jnp.log(filtered) * LOG10E).T
                sendbuf[r, :, :, half_row] = level.astype(BF16).reshape(ndate, 16, 128)
            send(r)

    def spread_step(waits):
        def body(i, carry):
            if waits:
                @pl.when(i < ROWS)
                def _():
                    for copy in loads(i - 3):
                        copy.wait()
            spread(i)
            return carry

        return body

    def take(rows):
        for r in rows:
            pltpu.make_async_copy(got.at[r, 0 : ndate - 1], got.at[r, 0 : ndate - 1], recv_sem.at[r]).wait()
            pltpu.make_async_copy(sendbuf.at[r, date], got.at[r, date], own_sem.at[r]).wait()
        total = acc[:, :128]
        for r in rows:
            series = got[r].reshape(ndate * 16, width)
            total = total + lax.dot_general(onehot[r], series, (((1,), (1,)), ((), ())), preferred_element_type=F32)
        acc[:, :128] = total

    lax.fori_loop(3, 12, spread_step(True), 0)
    pl.semaphore_wait(barrier, degree)
    halo_out()
    group([3, 4, 5], init=True)
    lax.fori_loop(12, 16, spread_step(True), 0)
    group([6, 7, 8, 9])
    lax.fori_loop(16, ROWS + 3, spread_step(True), 0)
    group([10, 11, 12])
    take(range(3, 6))

    @pl.when(space < nspace - 1)
    def _():
        up().wait_recv()
        unpack(1, ROWS + 3)

    lax.fori_loop(ROWS + 3, ROWS + 6, spread_step(False), 0)
    group([13, 14, 15])
    take(range(6, 9))

    @pl.when(space > 0)
    def _():
        down().wait_recv()
        unpack(0, 0)

    lax.fori_loop(0, 3, spread_step(False), 0)
    group([2, 1, 0])
    take(range(9, ROWS))
    take(range(3))

    high = date // half
    low = lax.rem(space, 2)
    copies = []
    for k in range(1, 4):
        far, near = k // 2, k % 2
        part = lax.rem(high + far, 2) * 2 + lax.rem(low + near, 2)
        copy = pltpu.make_async_remote_copy(
            src_ref=acc.at[pl.ds(pl.multiple_of(part * ROWS, ROWS), ROWS)], dst_ref=qgot.at[k - 1],
            send_sem=qsend.at[k - 1], recv_sem=qrecv.at[k - 1],
            device_id={"date": opposite if far else date, "space": mate if near else space}, device_id_type=MESH)
        copy.start()
        copies.append(copy)

    total = acc[pl.ds(pl.multiple_of((high * 2 + low) * ROWS, ROWS), ROWS), :]
    for k, copy in enumerate(copies):
        copy.wait_recv()
        total = total + qgot[k]
    total_ref[...] = total

    for copy in copies:
        copy.wait_send()
    pltpu.make_async_copy(sendbuf.at[:, 0 : ndate - 1], sendbuf.at[:, 0 : ndate - 1], send_sem).wait()

    @pl.when(space < nspace - 1)
    def _():
        down().wait_send()

    @pl.when(space > 0)
    def _():
        up().wait_send()


def fit_kernel(got, total_ref, basis_ref, out_hbm, means_ref, out, out_sem):
    def copy(r):
        return pltpu.make_async_copy(out.at[r], out_hbm.at[r], out_sem.at[r])

    for r in range(ROWS):
        series = got[r].reshape(basis_ref.shape[0], got.shape[3])
        coeffs = lax.dot_general(series, basis_ref[...], (((0,), (0,)), ((), ())), preferred_element_type=F32)
        out[r] = coeffs.astype(BF16)
        copy(r).start()
    sums, counts = total_ref[:, :128], total_ref[:, 128:]
    coarse = sums.astype(BF16)
    fine = (sums - coarse.astype(F32)).astype(BF16)
    sums = jnp.dot(coarse, basis_ref[...], preferred_element_type=F32) + jnp.dot(fine, basis_ref[...], preferred_element_type=F32)
    means_ref[...] = sums / jnp.maximum(counts, 1.0)
    for r in range(ROWS):
        copy(r).wait()


def solution(mesh):
    ndate, nspace = mesh.shape["date"], mesh.shape["space"]
    basis = basis_table(DATES, DATES // ndate, 2)

    def local(backscatter, edge_dirs, labels, parcel_slot):
        wide = backscatter.shape[3]
        cols = wide // ndate
        hbm = pl.BlockSpec(memory_space=pltpu.HBM)
        vmem = pl.BlockSpec(memory_space=pltpu.VMEM)
        got, total = pl.pallas_call(
            functools.partial(kernel, ndate, nspace, wide),
            out_shape=(
                jax.ShapeDtypeStruct((ROWS, ndate, 16, cols), BF16),
                jax.ShapeDtypeStruct((ROWS, 256), F32),
            ),
            in_specs=[hbm] * 4,
            out_specs=(vmem, vmem),
            scratch_shapes=[
                pltpu.VMEM((TALL, 2, 8, wide), F32),
                pltpu.VMEM((ROWS, 8, wide), jnp.int32),
                pltpu.VMEM((2, TALL, TALLER, 128), F32),
                pltpu.VMEM((2, TALL, 264, 128), F32),
                pltpu.VMEM((2, TALL, 256, 128), F32),
                pltpu.VMEM((GROUP, 2, 2, TALLER, 128), F32),
                pltpu.VMEM((GROUP, 2, 256, 128), F32),
                pltpu.VMEM((2, 4, 256, 128), F32),
                pltpu.VMEM((2, 4, 256, 128), F32),
                pltpu.VMEM((GROUP, 256, 128), jnp.int32),
                pltpu.VMEM((ROWS, ndate, 16, cols), BF16),
                pltpu.VMEM((ROWS, 4 * ROWS, cols), BF16),
                pltpu.VMEM((4 * ROWS, 256), F32),
                pltpu.VMEM((3, ROWS, 256), F32),
                pltpu.VMEM(labels.shape, jnp.int32),
                pltpu.VMEM((parcel_slot.shape[0] // 128, 128), jnp.int32),
                pltpu.VMEM((2, 3, 16, wide), jnp.int16),
                pltpu.VMEM((2, 3, 16, wide), jnp.int16),
                pltpu.SemaphoreType.DMA((ROWS, 3)),
                pltpu.SemaphoreType.DMA((2,)),
                pltpu.SemaphoreType.DMA((2,)),
                pltpu.SemaphoreType.DMA((2,)),
                pltpu.SemaphoreType.DMA,
                pltpu.SemaphoreType.DMA((ROWS,)),
                pltpu.SemaphoreType.DMA((ROWS,)),
                pltpu.SemaphoreType.DMA((3,)),
                pltpu.SemaphoreType.DMA((3,)),
            ],
            compiler_params=pltpu.CompilerParams(
                collective_id=0, has_side_effects=True, vmem_limit_bytes=44 * 1024 * 1024
            ),
        )(*[
            pltpu.with_memory_space_constraint(v, pltpu.HBM)
            for v in (backscatter, edge_dirs, labels, parcel_slot.reshape(-1, 128))
        ])
        return pl.pallas_call(
            fit_kernel,
            out_shape=(
                jax.ShapeDtypeStruct((ROWS, cols, 128), BF16),
                jax.ShapeDtypeStruct((ROWS, 128), F32),
            ),
            in_specs=[vmem] * 3,
            out_specs=(hbm, vmem),
            scratch_shapes=[pltpu.VMEM((ROWS, cols, 128), BF16), pltpu.SemaphoreType.DMA((ROWS,))],
            compiler_params=pltpu.CompilerParams(vmem_limit_bytes=8 * 1024 * 1024),
        )(got, total, jnp.asarray(basis))

    return jax.shard_map(
        local,
        mesh=mesh,
        in_specs=(P("date", None, "space", None), P("date", "space", None), P("space", "date"), P()),
        out_specs=(P("space", "date", None), P(("date", "space"), None)),
        check_vma=False,
    )
```

```python
import functools

import jax
import jax.numpy as jnp
import ml_dtypes
import numpy as np
from jax import lax
from jax.experimental import pallas as pl
from jax.experimental.pallas import tpu as pltpu
from jax.sharding import PartitionSpec as P

MESH = pl.DeviceIdType.MESH
F32 = jnp.float32
BF16 = jnp.bfloat16
DATES = 64
ROWS = 16
TALL = ROWS + 6
GROUP = 4
FAR_FIRST = (4, 3, 5, 2, 6, 1, 7)
LOG10E = 0.4342944819032518
STEPS = 65535.0
MIDDLE = 32768.0
LEFT = 24
TALLER = LEFT + 256 + 24


def basis_table(dates, group, pols):
    times = np.arange(dates, dtype=np.float32)[:, None]
    index = np.arange(dates, dtype=np.float32)[None, :]
    half = dates // 2
    scale = np.sqrt(np.float32(2.0 / dates))
    cosine = np.cos(np.float32(2.0 * np.pi) * index * times / np.float32(dates))
    sine = np.sin(np.float32(2.0 * np.pi) * (index - half) * times / np.float32(dates))
    table = (np.where(index <= half, cosine, sine) * scale).astype(np.float32)
    wide = np.zeros((dates // group, pols, group, pols, dates), np.float32)
    for p in range(pols):
        wide[:, p, :, p, :] = table.reshape(dates // group, group, dates)
    return wide.reshape(dates * pols, pols * dates).astype(ml_dtypes.bfloat16)


def kernel(
    ndate, nspace, wide,
    x_hbm, e_hbm, labels_hbm, slot_hbm, basis_hbm,
    coeffs_ref, total_ref,
    xin, ein, yy, a0, r7, dd, ff, ahead, behind, ey, sendbuf, got, onehot, acc, qgot, labels_ref, slot_ref, basis_ref, edge_out, edge_in,
    in_sem, small_sem, halo_send, halo_recv, send_sem, recv_sem, own_sem, qsend, qrecv,
):
    date = lax.axis_index("date")
    space = lax.axis_index("space")
    half = ndate // 2

    order = list(range(9)) + list(range(ROWS - 3, ROWS)) + list(range(9, ROWS - 3))

    def loads(r):
        for p in range(2):
            yield pltpu.make_async_copy(x_hbm.at[:, p, r, :], xin.at[r + 3, p], in_sem.at[r, p])
        yield pltpu.make_async_copy(e_hbm.at[:, r, :], ein.at[r], in_sem.at[r, 2])

    small = [
        pltpu.make_async_copy(source, target, small_sem.at[n])
        for n, (source, target) in enumerate(
            ((slot_hbm, slot_ref), (labels_hbm, labels_ref), (basis_hbm, basis_ref)))
    ]
    for copy in small:
        copy.start()
    for r in order:
        for copy in loads(r):
            copy.start()

    barrier = pltpu.get_barrier_semaphore()
    for k in range(1, ndate):
        pl.semaphore_signal(barrier, inc=1, device_id={"date": lax.rem(date + k, ndate)}, device_id_type=MESH)
    mate = space + 1 - 2 * lax.rem(space, 2)
    opposite = lax.rem(date + half, ndate)
    pl.semaphore_signal(barrier, inc=1, device_id={"date": opposite, "space": mate}, device_id_type=MESH)

    @pl.when(space > 0)
    def _():
        pl.semaphore_signal(barrier, inc=1, device_id={"space": space - 1}, device_id_type=MESH)

    @pl.when(space < nspace - 1)
    def _():
        pl.semaphore_signal(barrier, inc=1, device_id={"space": space + 1}, device_id_type=MESH)

    def down():
        return pltpu.make_async_remote_copy(
            src_ref=edge_out.at[1], dst_ref=edge_in.at[0],
            send_sem=halo_send.at[0], recv_sem=halo_recv.at[0],
            device_id={"space": space + 1}, device_id_type=MESH)

    def up():
        return pltpu.make_async_remote_copy(
            src_ref=edge_out.at[0], dst_ref=edge_in.at[1],
            send_sem=halo_send.at[1], recv_sem=halo_recv.at[1],
            device_id={"space": space - 1}, device_id_type=MESH)

    def pack(side, first):
        for k in range(3):
            x = xin[first + k].reshape(16, wide)
            edge_out[side, k] = ((x * STEPS + 0.5).astype(jnp.int32) - 32768).astype(jnp.int16)

    def unpack(side, first):
        for k in range(3):
            x = (edge_in[side, k].astype(jnp.int32).astype(F32) + MIDDLE) * (1.0 / STEPS)
            xin[first + k] = x.reshape(2, 8, wide)

    def halo_out():
        for r in range(ROWS - 3, ROWS):
            for copy in loads(r):
                copy.wait()
        pack(0, 3)
        pack(1, ROWS)

        @pl.when(space < nspace - 1)
        def _():
            down().start()

        @pl.when(space > 0)
        def _():
            up().start()

    degree = (ndate - 1) + 1 + jnp.where(space > 0, 1, 0) + jnp.where(space < nspace - 1, 1, 0)

    @pl.when(space == 0)
    def _():
        xin[0:3] = jnp.zeros((3, 2, 8, wide), F32)

    @pl.when(space == nspace - 1)
    def _():
        xin[ROWS + 3 : ROWS + 6] = jnp.zeros((3, 2, 8, wide), F32)

    def send(r):
        for k in FAR_FIRST:
            peer = lax.rem(date + k, ndate)
            pltpu.make_async_remote_copy(
                src_ref=sendbuf.at[r, peer], dst_ref=got.at[r, date],
                send_sem=send_sem, recv_sem=recv_sem.at[r],
                device_id={"date": peer}, device_id_type=MESH).start()
        pltpu.make_async_copy(sendbuf.at[r, date], got.at[r, date], own_sem.at[r]).start()

    lanes = lax.broadcasted_iota(jnp.int32, (16, 128), 1)
    width = wide // ndate

    def spread(i):
        halves = []
        for h in range(2):
            tiles = [xin[i, p, :, b * width + h * 128 : b * width + (h + 1) * 128] for b in range(ndate) for p in range(2)]
            half_row = jnp.concatenate(tiles, axis=0).T
            yy[0, i, LEFT + h * 128 : LEFT + (h + 1) * 128] = half_row
            halves.append(half_row)
        before = pltpu.roll(halves[1][112:], 16, axis=1)
        after = pltpu.roll(halves[0][:16], 112, axis=1)
        yy[0, i, LEFT - 16 : LEFT] = jnp.where(lanes >= 16, before, 0.0)
        yy[0, i, LEFT + 256 : LEFT + 272] = jnp.where(lanes < 112, after, 0.0)
        for at, size in ((LEFT - 16, 8), (LEFT + 256, 16)):
            x = yy[0, i, at : at + size]
            yy[1, i, at : at + size] = x * x
        for n in range(4):
            start, size = (0, 72) if n == 0 else (8 + 64 * n, 64)
            at = LEFT - 8 + start
            shifted = [yy[0, i, at + k : at + k + size] for k in range(4)]
            for q in range(2):
                if q:
                    shifted = [x * x for x in shifted]
                    yy[1, i, at : at + size] = shifted[0]
                four = (shifted[0] + shifted[1]) + (shifted[2] + shifted[3])
                a0[q, i, start : start + size] = four
                skip = 8 if n == 0 else 0
                r7[q, i, 64 * n : 64 * n + 64] = (
                    four[skip:] + a0[q, i, start + skip - 3 : start + size - 3] - shifted[0][skip:]
                )

    def diagonals(rows):
        for n, r in enumerate(sorted(rows)):
            for q in range(2):
                for k in range(2):
                    side = -1 if k == 0 else 1
                    for m in range(3):
                        at = LEFT - 8 * k + 88 * m

                        def x(i, off):
                            return yy[q, i, at + off : at + off + 88]

                        if n == 0:
                            total = x(r, -3 * side)
                            for i in range(1, 7):
                                total = total + x(r + i, (i - 3) * side)
                        else:
                            total = dd[n - 1, q, k, at - side : at - side + 88] - x(r - 1, -4 * side) + x(r + 6, 3 * side)
                        dd[n, q, k, at : at + 88] = total

    def windows(rows, init):
        step = rows[1] - rows[0]

        def tile(t, carry):
            at = pl.multiple_of(t * 8, 8)
            here = pl.ds(at, 8)
            pairs, quads, state, cols = {}, {}, {}, {}

            def x(q, i, off):
                return yy[q, i, pl.ds(at + LEFT + off, 8), :]

            def row(q, i):
                return r7[q, i, here, :]

            def pair(q, i):
                if (q, i) not in pairs:
                    pairs[q, i] = row(q, i) + row(q, i + 1)
                return pairs[q, i]

            def quad(q, i):
                if (q, i) not in quads:
                    quads[q, i] = pair(q, i) + pair(q, i + 2)
                return quads[q, i]

            def start(q, r):
                total = [None] * 4
                for k in range(-3, 4):
                    i, m = r + 3 + k, abs(k)
                    four, ruof = a0[q, i, pl.ds(at + 8, 8), :], a0[q, i, pl.ds(at + 5, 8), :]
                    if m == 0:
                        parts = (four, four, ruof, ruof)
                    elif m == 1:
                        mid = x(q, i, 0)
                        parts = (four + x(q, i, -1), four - mid, ruof - mid, ruof + x(q, i, 1))
                    elif m == 2:
                        whole, low, high = row(q, i), x(q, i, -3), x(q, i, 3)
                        parts = (whole - low, high + x(q, i, 2), low + x(q, i, -2), whole - high)
                    else:
                        whole = row(q, i)
                        parts = (whole, x(q, i, 3), x(q, i, -3), whole)
                    if k < 0:
                        parts = (parts[1], parts[0], parts[3], parts[2])
                    total = [p if t is None else t + p for t, p in zip(total, parts)]
                return total

            for n, r in enumerate(rows):
                e = ey[n, here, :]
                b0 = (e & 1) > 0
                b1 = (e & 2) > 0
                b2 = e > 3
                for q in range(2):
                    slot = sorted(rows).index(r)
                    d1 = dd[slot, q, 0, pl.ds(at + LEFT, 8), :]
                    d2 = dd[slot, q, 1, pl.ds(at + LEFT, 8), :]
                    if n == 0 and init:
                        t1, t3, t5, t7 = start(q, r)
                        for k, value in enumerate((t1, t3 - d2, t5 - d1, t7)):
                            behind[q, k, here, :] = value
                        state[q] = (t1 - d1, t3, t5, t7 - d2)
                    else:
                        if n == 0:
                            state[q] = [(ahead if step > 0 else behind)[q, k, here, :] for k in range(4)]
                        t1, t3, t5, t7 = state[q]
                        if step > 0:
                            new, old = row(q, r + 6), row(q, r - 1)
                            t1, t7 = t1 + new, t7 + new
                            t3, t5 = t3 + d2 - old, t5 + d1 - old
                            state[q] = (t1 - d1, t3, t5, t7 - d2)
                        else:
                            new, old = row(q, r), row(q, r + 7)
                            t3, t5 = t3 + new, t5 + new
                            t1, t7 = t1 + d1 - old, t7 + d2 - old
                            state[q] = (t1, t3 - d2, t5 - d1, t7)
                    if n == 0:
                        both = []
                        for off in (8, 5):
                            total = a0[q, r, pl.ds(at + off, 8), :]
                            for i in range(1, 7):
                                total = total + a0[q, r + i, pl.ds(at + off, 8), :]
                            both.append(total)
                    else:
                        new, old = (r + 6, r - 1) if step > 0 else (r, r + 7)
                        both = [
                            total + a0[q, new, pl.ds(at + off, 8), :] - a0[q, old, pl.ds(at + off, 8), :]
                            for total, off in zip(cols[q], (8, 5))
                        ]
                    cols[q] = both
                    s02 = jnp.where(b1, both[0], quad(q, r + 3))
                    s46 = jnp.where(b1, both[1], quad(q, r))
                    s13 = jnp.where(b1, t3, t1)
                    s57 = jnp.where(b1, t7, t5)
                    ff[n, q, here, :] = jnp.where(b2, jnp.where(b0, s57, s46), jnp.where(b0, s13, s02))
            if step > 0:
                for q in range(2):
                    for k in range(4):
                        ahead[q, k, here, :] = state[q][k]
            return carry

        lax.fori_loop(0, 8, lambda t, c: tile(4 * t + 3, tile(4 * t + 2, tile(4 * t + 1, tile(4 * t, c)))), 0)

    def group(rows, init=False):
        for n, r in enumerate(rows):
            for h in range(2):
                tiles = [ein[r, :, b * width + h * 128 : b * width + (h + 1) * 128] for b in range(ndate) for p in range(2)]
                ey[n, h * 128 : (h + 1) * 128] = jnp.concatenate(tiles, axis=0).T
        diagonals(rows)
        windows(rows, init)
        for n, r in enumerate(rows):
            for h in range(2):
                half_row = slice(h * 128, (h + 1) * 128)
                x = yy[0, r + 3, LEFT + h * 128 : LEFT + (h + 1) * 128]
                mean = ff[n, 0, half_row] * (1.0 / 28.0)
                sq_mean = mean * mean
                excess = jnp.maximum(ff[n, 1, half_row] * (1.0 / 28.0) - 1.25 * sq_mean, 0.0)
                under = excess + 0.3125 * sq_mean
                inv = pl.reciprocal(under, approx=True)
                filtered = mean + excess * inv * (x - mean)
                level = (jnp.log(filtered) * LOG10E).astype(BF16).T
                sendbuf[r, :, :, half_row] = level.reshape(ndate, 16, 128)
            send(r)

    def spread_step(waits):
        def body(i, carry):
            if waits:
                @pl.when(i < ROWS)
                def _():
                    for copy in loads(i - 3):
                        copy.wait()
            spread(i)
            return carry

        return body

    def take(rows):
        for r in rows:
            pltpu.make_async_copy(got.at[r, 0 : ndate - 1], got.at[r, 0 : ndate - 1], recv_sem.at[r]).wait()
            pltpu.make_async_copy(sendbuf.at[r, date], got.at[r, date], own_sem.at[r]).wait()
        total = acc[:, :128]
        for r in rows:
            series = got[r].reshape(ndate * 16, width)
            total = total + lax.dot_general(onehot[r], series, (((1,), (1,)), ((), ())), preferred_element_type=F32)
        acc[:, :128] = total

    lax.fori_loop(3, 12, spread_step(True), 0, unroll=True)
    pl.semaphore_wait(barrier, degree)
    halo_out()
    group([3, 4, 5], init=True)
    lax.fori_loop(12, 16, spread_step(True), 0, unroll=True)
    group([6, 7, 8, 9])
    lax.fori_loop(16, ROWS + 3, spread_step(True), 0, unroll=True)
    group([10, 11, 12])

    @pl.when(space < nspace - 1)
    def _():
        up().wait_recv()
        unpack(1, ROWS + 3)

    lax.fori_loop(ROWS + 3, ROWS + 6, spread_step(False), 0, unroll=True)
    group([13, 14, 15])

    @pl.when(space > 0)
    def _():
        down().wait_recv()
        unpack(0, 0)

    lax.fori_loop(0, 3, spread_step(False), 0, unroll=True)
    group([2, 1, 0])

    for copy in small:
        copy.wait()

    base_date = lax.rem(date, half)
    base_space = space - lax.rem(space, 2)
    parts = []
    for u in range(4):
        owner = (base_date + (u // 2) * half) * nspace + base_space + u % 2
        parts.append(lax.broadcasted_iota(jnp.int32, (ROWS, 128), 0) + owner * ROWS)
    ids = jnp.concatenate(parts, axis=0)
    lane = lax.broadcasted_iota(jnp.int32, (4 * ROWS, 128), 1).astype(F32)
    total = jnp.zeros((4 * ROWS, 128), F32)
    for g in range(slot_ref.shape[0]):
        total = total + jnp.where(ids == slot_ref[g : g + 1, :], lane + float(128 * g), 0.0)
    parcel_of = jnp.sum(total, axis=1, keepdims=True).astype(jnp.int32)
    for r in range(ROWS):
        onehot[r] = jnp.where(parcel_of == labels_ref[r : r + 1, :], 1.0, 0.0).astype(BF16)

    present = onehot[0].astype(F32)
    for r in range(1, ROWS):
        present = present + onehot[r].astype(F32)
    acc[:, :128] = jnp.zeros((4 * ROWS, 128), F32)
    acc[:, 128:] = jnp.broadcast_to(jnp.sum(present, axis=1, keepdims=True), (4 * ROWS, 128))

    take(range(3, ROWS))
    take(range(3))

    high = date // half
    low = lax.rem(space, 2)
    copies = []
    for k in range(1, 4):
        far, near = k // 2, k % 2
        part = lax.rem(high + far, 2) * 2 + lax.rem(low + near, 2)
        copy = pltpu.make_async_remote_copy(
            src_ref=acc.at[pl.ds(pl.multiple_of(part * ROWS, ROWS), ROWS)], dst_ref=qgot.at[k - 1],
            send_sem=qsend.at[k - 1], recv_sem=qrecv.at[k - 1],
            device_id={"date": opposite if far else date, "space": mate if near else space}, device_id_type=MESH)
        copy.start()
        copies.append(copy)

    for r in range(ROWS):
        series = got[r].reshape(ndate * 16, width)
        coeffs = lax.dot_general(series, basis_ref[...], (((0,), (0,)), ((), ())), preferred_element_type=F32)
        coeffs_ref[r] = coeffs.astype(BF16)

    total = acc[pl.ds(pl.multiple_of((high * 2 + low) * ROWS, ROWS), ROWS), :]
    for k, copy in enumerate(copies):
        copy.wait_recv()
        total = total + qgot[k]
    total_ref[...] = total

    for copy in copies:
        copy.wait_send()
    pltpu.make_async_copy(sendbuf.at[:, 0 : ndate - 1], sendbuf.at[:, 0 : ndate - 1], send_sem).wait()

    @pl.when(space < nspace - 1)
    def _():
        down().wait_send()

    @pl.when(space > 0)
    def _():
        up().wait_send()


def finish(coeffs_ref, total_ref, basis_ref, out_hbm, means_ref, out_sem):
    copies = [
        pltpu.make_async_copy(coeffs_ref.at[4 * n : 4 * n + 4], out_hbm.at[4 * n : 4 * n + 4], out_sem.at[n])
        for n in range(ROWS // 4)
    ]
    for copy in copies:
        copy.start()
    sums, counts = total_ref[:, :128], total_ref[:, 128:]
    coarse = sums.astype(BF16)
    fine = (sums - coarse.astype(F32)).astype(BF16)
    sums = jnp.dot(coarse, basis_ref[...], preferred_element_type=F32) + jnp.dot(fine, basis_ref[...], preferred_element_type=F32)
    means_ref[...] = sums / jnp.maximum(counts, 1.0)
    for copy in copies:
        copy.wait()


def solution(mesh):
    ndate, nspace = mesh.shape["date"], mesh.shape["space"]
    basis = basis_table(DATES, DATES // ndate, 2)

    def local(backscatter, edge_dirs, labels, parcel_slot):
        wide = backscatter.shape[3]
        cols = wide // ndate
        hbm = pl.BlockSpec(memory_space=pltpu.HBM)
        vmem = pl.BlockSpec(memory_space=pltpu.VMEM)
        coeffs, total = pl.pallas_call(
            functools.partial(kernel, ndate, nspace, wide),
            out_shape=(
                jax.ShapeDtypeStruct((ROWS, cols, 128), BF16),
                jax.ShapeDtypeStruct((ROWS, 256), F32),
            ),
            in_specs=[hbm] * 5,
            out_specs=(vmem, vmem),
            scratch_shapes=[
                pltpu.VMEM((TALL, 2, 8, wide), F32),
                pltpu.VMEM((ROWS, 8, wide), jnp.int32),
                pltpu.VMEM((2, TALL, TALLER, 128), F32),
                pltpu.VMEM((2, TALL, 264, 128), F32),
                pltpu.VMEM((2, TALL, 256, 128), F32),
                pltpu.VMEM((GROUP, 2, 2, TALLER, 128), F32),
                pltpu.VMEM((GROUP, 2, 256, 128), F32),
                pltpu.VMEM((2, 4, 256, 128), F32),
                pltpu.VMEM((2, 4, 256, 128), F32),
                pltpu.VMEM((GROUP, 256, 128), jnp.int32),
                pltpu.VMEM((ROWS, ndate, 16, cols), BF16),
                pltpu.VMEM((ROWS, ndate, 16, cols), BF16),
                pltpu.VMEM((ROWS, 4 * ROWS, cols), BF16),
                pltpu.VMEM((4 * ROWS, 256), F32),
                pltpu.VMEM((3, ROWS, 256), F32),
                pltpu.VMEM(labels.shape, jnp.int32),
                pltpu.VMEM((parcel_slot.shape[0] // 128, 128), jnp.int32),
                pltpu.VMEM(basis.shape, BF16),
                pltpu.VMEM((2, 3, 16, wide), jnp.int16),
                pltpu.VMEM((2, 3, 16, wide), jnp.int16),
                pltpu.SemaphoreType.DMA((ROWS, 3)),
                pltpu.SemaphoreType.DMA((3,)),
                pltpu.SemaphoreType.DMA((2,)),
                pltpu.SemaphoreType.DMA((2,)),
                pltpu.SemaphoreType.DMA,
                pltpu.SemaphoreType.DMA((ROWS,)),
                pltpu.SemaphoreType.DMA((ROWS,)),
                pltpu.SemaphoreType.DMA((3,)),
                pltpu.SemaphoreType.DMA((3,)),
            ],
            compiler_params=pltpu.CompilerParams(
                collective_id=0, has_side_effects=True, vmem_limit_bytes=44 * 1024 * 1024
            ),
        )(*[
            pltpu.with_memory_space_constraint(v, pltpu.HBM)
            for v in (backscatter, edge_dirs, labels, parcel_slot.reshape(-1, 128), jnp.asarray(basis))
        ])
        return pl.pallas_call(
            finish,
            out_shape=(
                jax.ShapeDtypeStruct((ROWS, cols, 128), BF16),
                jax.ShapeDtypeStruct((ROWS, 128), F32),
            ),
            in_specs=[vmem] * 3,
            out_specs=(hbm, vmem),
            scratch_shapes=[pltpu.SemaphoreType.DMA((ROWS // 4,))],
            compiler_params=pltpu.CompilerParams(vmem_limit_bytes=8 * 1024 * 1024),
        )(coeffs, total, jnp.asarray(basis))

    return jax.shard_map(
        local,
        mesh=mesh,
        in_specs=(P("date", None, "space", None), P("date", "space", None), P("space", "date"), P()),
        out_specs=(P("space", "date", None), P(("date", "space"), None)),
        check_vma=False,
    )
```

```python
import functools

import jax
import jax.numpy as jnp
import ml_dtypes
import numpy as np
from jax import lax
from jax.experimental import pallas as pl
from jax.experimental.pallas import tpu as pltpu
from jax.sharding import PartitionSpec as P

MESH = pl.DeviceIdType.MESH
F32 = jnp.float32
BF16 = jnp.bfloat16
DATES = 64
ROWS = 16
TALL = ROWS + 6
GROUP = 4
FAR_FIRST = (4, 3, 5, 2, 6, 1, 7)
GROUPS = ((3, 4, 5), (6, 7, 8, 9), (10, 11, 12), (13, 14, 15), (2, 1, 0))
LOG10E = 0.4342944819032518
STEPS = 65535.0
MIDDLE = 32768.0
LEFT = 24
TALLER = LEFT + 256 + 24


def basis_table(dates, group, pols):
    times = np.arange(dates, dtype=np.float32)[:, None]
    index = np.arange(dates, dtype=np.float32)[None, :]
    half = dates // 2
    scale = np.sqrt(np.float32(2.0 / dates))
    cosine = np.cos(np.float32(2.0 * np.pi) * index * times / np.float32(dates))
    sine = np.sin(np.float32(2.0 * np.pi) * (index - half) * times / np.float32(dates))
    table = (np.where(index <= half, cosine, sine) * scale).astype(np.float32)
    wide = np.zeros((dates // group, pols, group, pols, dates), np.float32)
    for p in range(pols):
        wide[:, p, :, p, :] = table.reshape(dates // group, group, dates)
    return wide.reshape(dates * pols, pols * dates).astype(ml_dtypes.bfloat16)


def kernel(
    ndate, nspace, wide,
    x_hbm, e_hbm, labels_hbm, slot_hbm, basis_hbm,
    coeffs_ref, total_ref,
    xin, ein, yy, a0, r7, dd, ff, ahead, behind, ey, sendbuf, got, onehot, acc, qgot, labels_ref, slot_ref, basis_ref, edge_out, edge_in,
    in_sem, small_sem, halo_send, halo_recv, send_sem, recv_sem, own_sem, qsend, qrecv,
):
    date = lax.axis_index("date")
    space = lax.axis_index("space")
    half = ndate // 2

    order = list(range(9)) + list(range(ROWS - 3, ROWS)) + list(range(9, ROWS - 3))

    def loads(r):
        for p in range(2):
            yield pltpu.make_async_copy(x_hbm.at[:, p, r, :], xin.at[r + 3, p], in_sem.at[r, p])
        yield pltpu.make_async_copy(e_hbm.at[:, r, :], ein.at[r], in_sem.at[r, 2])

    small = [
        pltpu.make_async_copy(source, target, small_sem.at[n])
        for n, (source, target) in enumerate(
            ((slot_hbm, slot_ref), (labels_hbm, labels_ref), (basis_hbm, basis_ref)))
    ]
    for copy in small:
        copy.start()
    for r in order:
        for copy in loads(r):
            copy.start()

    barrier = pltpu.get_barrier_semaphore()
    for k in range(1, ndate):
        pl.semaphore_signal(barrier, inc=1, device_id={"date": lax.rem(date + k, ndate)}, device_id_type=MESH)
    mate = space + 1 - 2 * lax.rem(space, 2)
    opposite = lax.rem(date + half, ndate)
    pl.semaphore_signal(barrier, inc=1, device_id={"date": opposite, "space": mate}, device_id_type=MESH)

    @pl.when(space > 0)
    def _():
        pl.semaphore_signal(barrier, inc=1, device_id={"space": space - 1}, device_id_type=MESH)

    @pl.when(space < nspace - 1)
    def _():
        pl.semaphore_signal(barrier, inc=1, device_id={"space": space + 1}, device_id_type=MESH)

    def down():
        return pltpu.make_async_remote_copy(
            src_ref=edge_out.at[1], dst_ref=edge_in.at[0],
            send_sem=halo_send.at[0], recv_sem=halo_recv.at[0],
            device_id={"space": space + 1}, device_id_type=MESH)

    def up():
        return pltpu.make_async_remote_copy(
            src_ref=edge_out.at[0], dst_ref=edge_in.at[1],
            send_sem=halo_send.at[1], recv_sem=halo_recv.at[1],
            device_id={"space": space - 1}, device_id_type=MESH)

    def pack(side, first):
        for k in range(3):
            x = xin[first + k].reshape(16, wide)
            edge_out[side, k] = ((x * STEPS + 0.5).astype(jnp.int32) - 32768).astype(jnp.int16)

    def unpack(side, first):
        for k in range(3):
            x = (edge_in[side, k].astype(jnp.int32).astype(F32) + MIDDLE) * (1.0 / STEPS)
            xin[first + k] = x.reshape(2, 8, wide)

    def halo_out():
        for r in range(ROWS - 3, ROWS):
            for copy in loads(r):
                copy.wait()
        pack(0, 3)
        pack(1, ROWS)

        @pl.when(space < nspace - 1)
        def _():
            down().start()

        @pl.when(space > 0)
        def _():
            up().start()

    degree = (ndate - 1) + 1 + jnp.where(space > 0, 1, 0) + jnp.where(space < nspace - 1, 1, 0)

    @pl.when(space == 0)
    def _():
        xin[0:3] = jnp.zeros((3, 2, 8, wide), F32)

    @pl.when(space == nspace - 1)
    def _():
        xin[ROWS + 3 : ROWS + 6] = jnp.zeros((3, 2, 8, wide), F32)

    def send(n, rows):
        here = pl.ds(min(rows), len(rows))
        for k in FAR_FIRST:
            peer = lax.rem(date + k, ndate)
            pltpu.make_async_remote_copy(
                src_ref=sendbuf.at[here, peer], dst_ref=got.at[here, date],
                send_sem=send_sem, recv_sem=recv_sem.at[n],
                device_id={"date": peer}, device_id_type=MESH).start()
        pltpu.make_async_copy(sendbuf.at[here, date], got.at[here, date], own_sem.at[n]).start()

    def arrive(n, rows):
        here = pl.ds(min(rows), len(rows))
        pltpu.make_async_copy(got.at[here, 0 : ndate - 1], got.at[here, 0 : ndate - 1], recv_sem.at[n]).wait()
        pltpu.make_async_copy(sendbuf.at[here, date], got.at[here, date], own_sem.at[n]).wait()

    lanes = lax.broadcasted_iota(jnp.int32, (16, 128), 1)
    width = wide // ndate

    def spread(i):
        halves = []
        for h in range(2):
            tiles = [xin[i, p, :, b * width + h * 128 : b * width + (h + 1) * 128] for b in range(ndate) for p in range(2)]
            half_row = jnp.concatenate(tiles, axis=0).T
            yy[0, i, LEFT + h * 128 : LEFT + (h + 1) * 128] = half_row
            halves.append(half_row)
        before = pltpu.roll(halves[1][112:], 16, axis=1)
        after = pltpu.roll(halves[0][:16], 112, axis=1)
        yy[0, i, LEFT - 16 : LEFT] = jnp.where(lanes >= 16, before, 0.0)
        yy[0, i, LEFT + 256 : LEFT + 272] = jnp.where(lanes < 112, after, 0.0)
        for at, size in ((LEFT - 16, 8), (LEFT + 256, 16)):
            x = yy[0, i, at : at + size]
            yy[1, i, at : at + size] = x * x
        for n in range(4):
            start, size = (0, 72) if n == 0 else (8 + 64 * n, 64)
            at = LEFT - 8 + start
            shifted = [yy[0, i, at + k : at + k + size] for k in range(4)]
            for q in range(2):
                if q:
                    shifted = [x * x for x in shifted]
                    yy[1, i, at : at + size] = shifted[0]
                four = (shifted[0] + shifted[1]) + (shifted[2] + shifted[3])
                a0[q, i, start : start + size] = four
                skip = 8 if n == 0 else 0
                r7[q, i, 64 * n : 64 * n + 64] = (
                    four[skip:] + a0[q, i, start + skip - 3 : start + size - 3] - shifted[0][skip:]
                )

    def diagonals(rows):
        for n, r in enumerate(sorted(rows)):
            for q in range(2):
                for k in range(2):
                    side = -1 if k == 0 else 1
                    for m in range(3):
                        at = LEFT - 8 * k + 88 * m

                        def x(i, off):
                            return yy[q, i, at + off : at + off + 88]

                        if n == 0:
                            total = x(r, -3 * side)
                            for i in range(1, 7):
                                total = total + x(r + i, (i - 3) * side)
                        else:
                            total = dd[n - 1, q, k, at - side : at - side + 88] - x(r - 1, -4 * side) + x(r + 6, 3 * side)
                        dd[n, q, k, at : at + 88] = total

    def windows(rows, init):
        step = rows[1] - rows[0]

        def tile(t, carry):
            at = pl.multiple_of(t * 8, 8)
            here = pl.ds(at, 8)
            pairs, quads, state, cols = {}, {}, {}, {}

            def x(q, i, off):
                return yy[q, i, pl.ds(at + LEFT + off, 8), :]

            def row(q, i):
                return r7[q, i, here, :]

            def pair(q, i):
                if (q, i) not in pairs:
                    pairs[q, i] = row(q, i) + row(q, i + 1)
                return pairs[q, i]

            def quad(q, i):
                if (q, i) not in quads:
                    quads[q, i] = pair(q, i) + pair(q, i + 2)
                return quads[q, i]

            def start(q, r):
                total = [None] * 4
                for k in range(-3, 4):
                    i, m = r + 3 + k, abs(k)
                    four, ruof = a0[q, i, pl.ds(at + 8, 8), :], a0[q, i, pl.ds(at + 5, 8), :]
                    if m == 0:
                        parts = (four, four, ruof, ruof)
                    elif m == 1:
                        mid = x(q, i, 0)
                        parts = (four + x(q, i, -1), four - mid, ruof - mid, ruof + x(q, i, 1))
                    elif m == 2:
                        whole, low, high = row(q, i), x(q, i, -3), x(q, i, 3)
                        parts = (whole - low, high + x(q, i, 2), low + x(q, i, -2), whole - high)
                    else:
                        whole = row(q, i)
                        parts = (whole, x(q, i, 3), x(q, i, -3), whole)
                    if k < 0:
                        parts = (parts[1], parts[0], parts[3], parts[2])
                    total = [p if t is None else t + p for t, p in zip(total, parts)]
                return total

            for n, r in enumerate(rows):
                e = ey[n, here, :]
                b0 = (e & 1) > 0
                b1 = (e & 2) > 0
                b2 = e > 3
                for q in range(2):
                    slot = sorted(rows).index(r)
                    d1 = dd[slot, q, 0, pl.ds(at + LEFT, 8), :]
                    d2 = dd[slot, q, 1, pl.ds(at + LEFT, 8), :]
                    if n == 0 and init:
                        t1, t3, t5, t7 = start(q, r)
                        for k, value in enumerate((t1, t3 - d2, t5 - d1, t7)):
                            behind[q, k, here, :] = value
                        state[q] = (t1 - d1, t3, t5, t7 - d2)
                    else:
                        if n == 0:
                            state[q] = [(ahead if step > 0 else behind)[q, k, here, :] for k in range(4)]
                        t1, t3, t5, t7 = state[q]
                        if step > 0:
                            new, old = row(q, r + 6), row(q, r - 1)
                            t1, t7 = t1 + new, t7 + new
                            t3, t5 = t3 + d2 - old, t5 + d1 - old
                            state[q] = (t1 - d1, t3, t5, t7 - d2)
                        else:
                            new, old = row(q, r), row(q, r + 7)
                            t3, t5 = t3 + new, t5 + new
                            t1, t7 = t1 + d1 - old, t7 + d2 - old
                            state[q] = (t1, t3 - d2, t5 - d1, t7)
                    if n == 0:
                        both = []
                        for off in (8, 5):
                            total = a0[q, r, pl.ds(at + off, 8), :]
                            for i in range(1, 7):
                                total = total + a0[q, r + i, pl.ds(at + off, 8), :]
                            both.append(total)
                    else:
                        new, old = (r + 6, r - 1) if step > 0 else (r, r + 7)
                        both = [
                            total + a0[q, new, pl.ds(at + off, 8), :] - a0[q, old, pl.ds(at + off, 8), :]
                            for total, off in zip(cols[q], (8, 5))
                        ]
                    cols[q] = both
                    s02 = jnp.where(b1, both[0], quad(q, r + 3))
                    s46 = jnp.where(b1, both[1], quad(q, r))
                    s13 = jnp.where(b1, t3, t1)
                    s57 = jnp.where(b1, t7, t5)
                    ff[n, q, here, :] = jnp.where(b2, jnp.where(b0, s57, s46), jnp.where(b0, s13, s02))
            if step > 0:
                for q in range(2):
                    for k in range(4):
                        ahead[q, k, here, :] = state[q][k]
            return carry

        lax.fori_loop(0, 8, lambda t, c: tile(4 * t + 3, tile(4 * t + 2, tile(4 * t + 1, tile(4 * t, c)))), 0)

    def group(number, init=False):
        rows = GROUPS[number]
        for n, r in enumerate(rows):
            for h in range(2):
                tiles = [ein[r, :, b * width + h * 128 : b * width + (h + 1) * 128] for b in range(ndate) for p in range(2)]
                ey[n, h * 128 : (h + 1) * 128] = jnp.concatenate(tiles, axis=0).T
        diagonals(rows)
        windows(rows, init)
        for n, r in enumerate(rows):
            for h in range(2):
                half_row = slice(h * 128, (h + 1) * 128)
                x = yy[0, r + 3, LEFT + h * 128 : LEFT + (h + 1) * 128]
                mean = ff[n, 0, half_row] * (1.0 / 28.0)
                sq_mean = mean * mean
                excess = jnp.maximum(ff[n, 1, half_row] * (1.0 / 28.0) - 1.25 * sq_mean, 0.0)
                under = excess + 0.3125 * sq_mean
                inv = pl.reciprocal(under, approx=True)
                filtered = mean + excess * inv * (x - mean)
                level = (jnp.log(filtered) * LOG10E).astype(BF16).T
                sendbuf[r, :, :, half_row] = level.reshape(ndate, 16, 128)
        send(number, rows)

    def spread_step(waits):
        def body(i, carry):
            if waits:
                @pl.when(i < ROWS)
                def _():
                    for copy in loads(i - 3):
                        copy.wait()
            spread(i)
            return carry

        return body

    def take(numbers):
        for n in numbers:
            arrive(n, GROUPS[n])
        rows = [r for n in numbers for r in GROUPS[n]]
        total = acc[:, :128]
        for r in rows:
            series = got[r].reshape(ndate * 16, width)
            total = total + lax.dot_general(onehot[r], series, (((1,), (1,)), ((), ())), preferred_element_type=F32)
        acc[:, :128] = total

    lax.fori_loop(3, 12, spread_step(True), 0, unroll=True)
    pl.semaphore_wait(barrier, degree)
    halo_out()
    group(0, init=True)
    lax.fori_loop(12, 16, spread_step(True), 0, unroll=True)
    group(1)
    lax.fori_loop(16, ROWS + 3, spread_step(True), 0, unroll=True)
    group(2)

    @pl.when(space < nspace - 1)
    def _():
        up().wait_recv()
        unpack(1, ROWS + 3)

    lax.fori_loop(ROWS + 3, ROWS + 6, spread_step(False), 0, unroll=True)
    group(3)

    @pl.when(space > 0)
    def _():
        down().wait_recv()
        unpack(0, 0)

    lax.fori_loop(0, 3, spread_step(False), 0, unroll=True)
    group(4)

    for copy in small:
        copy.wait()

    base_date = lax.rem(date, half)
    base_space = space - lax.rem(space, 2)
    parts = []
    for u in range(4):
        owner = (base_date + (u // 2) * half) * nspace + base_space + u % 2
        parts.append(lax.broadcasted_iota(jnp.int32, (ROWS, 128), 0) + owner * ROWS)
    ids = jnp.concatenate(parts, axis=0)
    lane = lax.broadcasted_iota(jnp.int32, (4 * ROWS, 128), 1).astype(F32)
    total = jnp.zeros((4 * ROWS, 128), F32)
    for g in range(slot_ref.shape[0]):
        total = total + jnp.where(ids == slot_ref[g : g + 1, :], lane + float(128 * g), 0.0)
    parcel_of = jnp.sum(total, axis=1, keepdims=True).astype(jnp.int32)
    for r in range(ROWS):
        onehot[r] = jnp.where(parcel_of == labels_ref[r : r + 1, :], 1.0, 0.0).astype(BF16)

    present = onehot[0].astype(F32)
    for r in range(1, ROWS):
        present = present + onehot[r].astype(F32)
    acc[:, :128] = jnp.zeros((4 * ROWS, 128), F32)
    acc[:, 128:] = jnp.broadcast_to(jnp.sum(present, axis=1, keepdims=True), (4 * ROWS, 128))

    take(range(4))
    take([4])

    high = date // half
    low = lax.rem(space, 2)
    copies = []
    for k in range(1, 4):
        far, near = k // 2, k % 2
        part = lax.rem(high + far, 2) * 2 + lax.rem(low + near, 2)
        copy = pltpu.make_async_remote_copy(
            src_ref=acc.at[pl.ds(pl.multiple_of(part * ROWS, ROWS), ROWS)], dst_ref=qgot.at[k - 1],
            send_sem=qsend.at[k - 1], recv_sem=qrecv.at[k - 1],
            device_id={"date": opposite if far else date, "space": mate if near else space}, device_id_type=MESH)
        copy.start()
        copies.append(copy)

    for r in range(ROWS):
        series = got[r].reshape(ndate * 16, width)
        coeffs = lax.dot_general(series, basis_ref[...], (((0,), (0,)), ((), ())), preferred_element_type=F32)
        coeffs_ref[r] = coeffs.astype(BF16)

    total = acc[pl.ds(pl.multiple_of((high * 2 + low) * ROWS, ROWS), ROWS), :]
    for k, copy in enumerate(copies):
        copy.wait_recv()
        total = total + qgot[k]
    total_ref[...] = total

    for copy in copies:
        copy.wait_send()
    pltpu.make_async_copy(sendbuf.at[:, 0 : ndate - 1], sendbuf.at[:, 0 : ndate - 1], send_sem).wait()

    @pl.when(space < nspace - 1)
    def _():
        down().wait_send()

    @pl.when(space > 0)
    def _():
        up().wait_send()


def finish(coeffs_ref, total_ref, basis_ref, out_hbm, means_ref, out_sem):
    copies = [
        pltpu.make_async_copy(coeffs_ref.at[4 * n : 4 * n + 4], out_hbm.at[4 * n : 4 * n + 4], out_sem.at[n])
        for n in range(ROWS // 4)
    ]
    for copy in copies:
        copy.start()
    sums, counts = total_ref[:, :128], total_ref[:, 128:]
    coarse = sums.astype(BF16)
    fine = (sums - coarse.astype(F32)).astype(BF16)
    sums = jnp.dot(coarse, basis_ref[...], preferred_element_type=F32) + jnp.dot(fine, basis_ref[...], preferred_element_type=F32)
    means_ref[...] = sums / jnp.maximum(counts, 1.0)
    for copy in copies:
        copy.wait()


def solution(mesh):
    ndate, nspace = mesh.shape["date"], mesh.shape["space"]
    basis = basis_table(DATES, DATES // ndate, 2)

    def local(backscatter, edge_dirs, labels, parcel_slot):
        wide = backscatter.shape[3]
        cols = wide // ndate
        hbm = pl.BlockSpec(memory_space=pltpu.HBM)
        vmem = pl.BlockSpec(memory_space=pltpu.VMEM)
        coeffs, total = pl.pallas_call(
            functools.partial(kernel, ndate, nspace, wide),
            out_shape=(
                jax.ShapeDtypeStruct((ROWS, cols, 128), BF16),
                jax.ShapeDtypeStruct((ROWS, 256), F32),
            ),
            in_specs=[hbm] * 5,
            out_specs=(vmem, vmem),
            scratch_shapes=[
                pltpu.VMEM((TALL, 2, 8, wide), F32),
                pltpu.VMEM((ROWS, 8, wide), jnp.int32),
                pltpu.VMEM((2, TALL, TALLER, 128), F32),
                pltpu.VMEM((2, TALL, 264, 128), F32),
                pltpu.VMEM((2, TALL, 256, 128), F32),
                pltpu.VMEM((GROUP, 2, 2, TALLER, 128), F32),
                pltpu.VMEM((GROUP, 2, 256, 128), F32),
                pltpu.VMEM((2, 4, 256, 128), F32),
                pltpu.VMEM((2, 4, 256, 128), F32),
                pltpu.VMEM((GROUP, 256, 128), jnp.int32),
                pltpu.VMEM((ROWS, ndate, 16, cols), BF16),
                pltpu.VMEM((ROWS, ndate, 16, cols), BF16),
                pltpu.VMEM((ROWS, 4 * ROWS, cols), BF16),
                pltpu.VMEM((4 * ROWS, 256), F32),
                pltpu.VMEM((3, ROWS, 256), F32),
                pltpu.VMEM(labels.shape, jnp.int32),
                pltpu.VMEM((parcel_slot.shape[0] // 128, 128), jnp.int32),
                pltpu.VMEM(basis.shape, BF16),
                pltpu.VMEM((2, 3, 16, wide), jnp.int16),
                pltpu.VMEM((2, 3, 16, wide), jnp.int16),
                pltpu.SemaphoreType.DMA((ROWS, 3)),
                pltpu.SemaphoreType.DMA((3,)),
                pltpu.SemaphoreType.DMA((2,)),
                pltpu.SemaphoreType.DMA((2,)),
                pltpu.SemaphoreType.DMA,
                pltpu.SemaphoreType.DMA((ROWS,)),
                pltpu.SemaphoreType.DMA((ROWS,)),
                pltpu.SemaphoreType.DMA((3,)),
                pltpu.SemaphoreType.DMA((3,)),
            ],
            compiler_params=pltpu.CompilerParams(
                collective_id=0, has_side_effects=True, vmem_limit_bytes=44 * 1024 * 1024
            ),
        )(*[
            pltpu.with_memory_space_constraint(v, pltpu.HBM)
            for v in (backscatter, edge_dirs, labels, parcel_slot.reshape(-1, 128), jnp.asarray(basis))
        ])
        return pl.pallas_call(
            finish,
            out_shape=(
                jax.ShapeDtypeStruct((ROWS, cols, 128), BF16),
                jax.ShapeDtypeStruct((ROWS, 128), F32),
            ),
            in_specs=[vmem] * 3,
            out_specs=(hbm, vmem),
            scratch_shapes=[pltpu.SemaphoreType.DMA((ROWS // 4,))],
            compiler_params=pltpu.CompilerParams(vmem_limit_bytes=8 * 1024 * 1024),
        )(coeffs, total, jnp.asarray(basis))

    return jax.shard_map(
        local,
        mesh=mesh,
        in_specs=(P("date", None, "space", None), P("date", "space", None), P("space", "date"), P()),
        out_specs=(P("space", "date", None), P(("date", "space"), None)),
        check_vma=False,
    )
```
